256 devices in a mesh: patch: 64 (over y, z, core), sub: 4 (over x).
Axes of the slice: x: 4, y: 4, z: 8, core: 2. Of those that a mesh axis runs over, the one named last changes fastest.
Arguments:
- positions: float32 [3, 8192, 128], P(None, 'patch'), may hold values from 0 to 24, as said below
- velocities: float32 [3, 8192, 128], P(None, 'patch'), may hold values from -0.3 to 0.3
- charges: float32 [8192, 128], P('patch'), may hold values from -1.2 to 1.2
- atom_type: int32 [8192, 128], P('patch'), may hold values from 0 to 7
- patch_fill: int32 [8192], P('patch'), may hold values from 8 to 128, as said below
- sigma_table: float32 [8], replicated, may hold values from 2.5 to 3.2
- eps_table: float32 [8], replicated, may hold values from 0.05 to 0.3
- inv_mass_table: float32 [8], replicated, may hold values from 0.3 to 1
- pair_first: int32 [64, 4, 896], P('patch', 'sub'), may hold values from 0 to 8191, as said below
- pair_second: int32 [64, 4, 896], P('patch', 'sub'), may hold values from -1 to 8191, as said below
Outputs:
- new_velocities: float32 [3, 8192, 128], P(None, 'patch')
- new_positions: float32 [3, 8192, 128], P(None, 'patch')
The draws below stay inside these ranges and needn't reach their ends.
Inputs may be any that keep to these rules, and one draw needn't show every extreme that they name: `positions`: every coordinate lies within its patch's cell; any two atoms, in one patch or in neighbouring ones, are 2.6 or more apart. `patch_fill`: some patch is full in every draw. All slots of device (g, s), live or not, have pair_first in one layer h, which is g - 1, g or g + 1 (modulo 64); for a live slot the cell step from pair_first to pair_second is (dx, dy, 1) with dx, dy in -1, 0, 1, or (0, 0, 0), (1, 0, 0), (-1, 1, 0), (0, 1, 0) or (1, 1, 0); every patch with itself and every two patches whose cells touch are in exactly one live slot; for each s, the slots whose pair_first lies in layer h sit on one device (., s). `pair_second`: same slots as pair_first; on each device the live slots come first and the unused ones hold -1; some device has all 896 slots live.
All inputs are finite; a program needn't handle non-finite values.
Results may differ from the reference program's by a relative error of at most 0.0003.
Values sent between devices are 32-bit elements; how exact they have to be, the bound alone decides.
A program may use at most 64 MiB of HBM per device.

```python
import math
import jax
import jax.numpy as jnp
from jax import lax

PATCH_ATOMS = 128
NTYPES = 8
PX = 8
PY = 16
P_DEV = 128
C_DEV = 896
GROUPS = 64
SUBS = 4
NPATCH = 8192


def pair_tables(key):
    keys = jax.random.split(key, 4)
    total_slots = 14 * P_DEV
    slot_index = jnp.arange(total_slots, dtype=jnp.int32)
    local_patch = slot_index // 14
    kind = slot_index % 14
    step_x = jnp.array([0, 1, -1, 0, 1, -1, 0, 1, -1, 0, 1, -1, 0, 1], jnp.int32)[kind]
    step_y = jnp.array([0, 0, 1, 1, 1, -1, -1, -1, 0, 0, 0, 1, 1, 1], jnp.int32)[kind]
    step_z = jnp.array([0, 0, 0, 0, 0, 1, 1, 1, 1, 1, 1, 1, 1, 1], jnp.int32)[kind]
    cell_x = local_patch % PX
    cell_y = local_patch // PX
    group_index = jnp.arange(GROUPS, dtype=jnp.int32)[:, None]
    second_local = (cell_x + step_x + PX) % PX + (cell_y + step_y + PY) % PY * PX
    firsts = group_index * P_DEV + local_patch[None, :]
    seconds = (group_index + step_z[None, :]) % GROUPS * P_DEV + second_local[None, :]
    ordering = jax.vmap(lambda sub_key: jax.random.permutation(sub_key, total_slots))(jax.random.split(keys[0], GROUPS)).astype(jnp.int32)
    firsts = jnp.take_along_axis(jnp.broadcast_to(firsts, ordering.shape), ordering, axis=1)
    seconds = jnp.take_along_axis(jnp.broadcast_to(seconds, ordering.shape), ordering, axis=1)
    heaviest = jax.random.randint(keys[1], (GROUPS,), 0, SUBS)
    remainder = total_slots - C_DEV
    cut_points = jnp.sort(jax.random.randint(keys[2], (GROUPS, SUBS - 2), 0, remainder + 1), axis=1)
    bounds = jnp.concatenate([jnp.zeros((GROUPS, 1), jnp.int32), cut_points.astype(jnp.int32), jnp.full((GROUPS, 1), remainder, jnp.int32)], axis=1)
    others = bounds[:, 1:] - bounds[:, :-1]
    sub_index = jnp.arange(SUBS, dtype=jnp.int32)[None, :]
    other_rank = jnp.clip(sub_index - (sub_index > heaviest[:, None]).astype(jnp.int32), 0, SUBS - 2)
    counts = jnp.where(sub_index == heaviest[:, None], C_DEV, jnp.take_along_axis(others, other_rank, axis=1))
    starts = jnp.cumsum(counts, axis=1) - counts
    column = jnp.arange(C_DEV, dtype=jnp.int32)
    active = column[None, None, :] < counts[:, :, None]
    placing = jnp.where(active, starts[:, :, None] + column[None, None, :], 0)
    group_rows = jnp.arange(GROUPS, dtype=jnp.int32)[:, None, None]
    filler = group_rows * P_DEV
    first_slots = jnp.where(active, firsts[group_rows, placing], filler)
    second_slots = jnp.where(active, seconds[group_rows, placing], -1)
    patterns = jnp.array([[0, 1, 2, 3], [1, 0, 2, 3], [0, 2, 1, 3], [0, 1, 3, 2], [1, 0, 3, 2]], jnp.int32)
    picks = jax.random.randint(keys[3], (SUBS, GROUPS // 4), 0, 5).at[0, 0].set(2)
    holder = jnp.arange(GROUPS, dtype=jnp.int32)
    source = holder // 4 * 4 + patterns[picks[:, holder // 4], holder % 4]
    sub_rows = jnp.arange(SUBS, dtype=jnp.int32)[:, None]
    first_out = jnp.transpose(first_slots[source, sub_rows], (1, 0, 2))
    second_out = jnp.transpose(second_slots[source, sub_rows], (1, 0, 2))
    return (first_out, second_out)


def draw_pair_first(key, part):
    return pair_tables(key)[0].astype(jnp.int32)


def draw_pair_second(key, part):
    return pair_tables(key)[1].astype(jnp.int32)


def draw_positions(key, part):
    key = jax.random.fold_in(key, 11)
    keys = jax.random.split(key, 2)
    atom_slot = jnp.arange(PATCH_ATOMS, dtype=jnp.int32)
    lattice = jnp.stack([atom_slot // 32, atom_slot // 8 % 4, atom_slot % 8]).astype(jnp.float32)
    anchor = (lattice + 0.5) * 3.0
    plane = atom_slot % 8
    layer = jnp.arange(NPATCH, dtype=jnp.int32) // P_DEV
    planes_moved = jax.random.uniform(keys[1], (2, GROUPS, 8), jnp.float32, -1.3, 1.3)
    lateral = planes_moved[:, layer][:, :, plane]
    moved = jnp.concatenate([lateral, jnp.zeros((1, NPATCH, PATCH_ATOMS), jnp.float32)], axis=0)
    uniform_part = jax.random.uniform(keys[0], (3, NPATCH, PATCH_ATOMS), jnp.float32, -1.0, 1.0)
    jitter = 0.2 * uniform_part
    return (anchor[:, None, :] + moved + jitter).astype(jnp.float32)


def draw_charges(key, part):
    key = jax.random.fold_in(key, 37)
    keys = jax.random.split(key, 2)
    plane = jnp.arange(PATCH_ATOMS, dtype=jnp.int32) % 8
    plane_sign = (2 * jax.random.randint(keys[0], (NPATCH, 8), 0, 2) - 1).astype(jnp.float32)
    signs = plane_sign[:, plane]
    size = jnp.minimum(jnp.abs(0.4 * jax.random.normal(keys[1], (NPATCH, PATCH_ATOMS), jnp.float32)), 1.2)
    return (signs * size).astype(jnp.float32)


def draw_patch_fill(key, part):
    key = jax.random.fold_in(key, 23)
    keys = jax.random.split(key, 3)
    patch_index = jnp.arange(NPATCH, dtype=jnp.int32)
    layer = patch_index // P_DEV
    liquid = layer * 5 // 3 % 2 == 0
    dense = jax.random.randint(keys[0], (NPATCH,), 97, PATCH_ATOMS + 1)
    sparse = jax.random.randint(keys[1], (NPATCH,), 8, 41)
    filled = jnp.where(liquid, dense, sparse)
    chosen = jax.random.randint(keys[2], (), 0, NPATCH)
    return jnp.where(patch_index == chosen, PATCH_ATOMS, filled).astype(jnp.int32)


def place_ends(result, stream_key, least, high):
    place = [jax.random.randint(jax.random.fold_in(stream_key, axis), (), 0, length) for axis, length in enumerate(result.shape)]
    widest = result.shape.index(max(result.shape))
    beside = place[:widest] + [(place[widest] + 1) % result.shape[widest]] + place[widest + 1:]
    return result.at[tuple(place)].set(least).at[tuple(beside)].set(high)


def steps_of(own_key, shape, cuts, smallest, top_value):
    gain = 1.0
    for dim, parts in cuts:
        heights = jax.random.uniform(jax.random.fold_in(jax.random.fold_in(own_key, 6), dim), (parts,), jnp.float32, smallest / len(cuts), top_value / len(cuts))
        gain = gain * jnp.repeat(jnp.exp(heights), shape[dim] // parts).reshape((-1,) + (1,) * (len(shape) - 1 - dim))
    return gain


def gaussian(rng, shape, spread, bound, cuts=(), kind=jnp.bfloat16):
    values = spread * jax.random.normal(rng, shape, jnp.float32)
    if cuts:
        values = values * steps_of(rng, shape, cuts, -0.22, 0.18)
    return jnp.clip(values, -bound, bound).astype(kind)


def setup_inputs(seed: int = 0) -> dict:
    splits = jax.random.split(jax.random.key(seed), 11)
    positions = draw_positions(jax.random.fold_in(splits[10], 71), 0)
    velocities = gaussian(splits[1], (3, NPATCH, PATCH_ATOMS), 0.05, 0.3, ((1, 64),), jnp.float32)
    charges = draw_charges(jax.random.fold_in(splits[10], 71), 0)
    atom_type = place_ends(jax.random.randint(splits[3], (NPATCH, PATCH_ATOMS), 0, NTYPES), jax.random.fold_in(splits[3], 1), 0, NTYPES - 1).astype(jnp.int32)
    patch_fill = draw_patch_fill(jax.random.fold_in(splits[10], 71), 0)
    sigma_table = jnp.clip(jax.random.uniform(splits[5], (NTYPES,), jnp.float32, 2.5, 3.2), 2.5, 3.2)
    eps_table = jnp.clip(jax.random.uniform(splits[6], (NTYPES,), jnp.float32, 0.05, 0.3), 0.05, 0.3)
    inv_mass_table = jnp.clip(jax.random.uniform(splits[7], (NTYPES,), jnp.float32, 0.3, 1.0), 0.3, 1.0)
    pair_first = draw_pair_first(jax.random.fold_in(splits[10], 71), 0)
    pair_second = draw_pair_second(jax.random.fold_in(splits[10], 71), 0)
    return {"positions": positions, "velocities": velocities, "charges": charges, "atom_type": atom_type, "patch_fill": patch_fill, "sigma_table": sigma_table, "eps_table": eps_table, "inv_mass_table": inv_mass_table, "pair_first": pair_first, "pair_second": pair_second}


COULOMB = 332.0636
SPLIT_BETA = 0.2
GAUSS_FACTOR = 2.0 * 0.2 / math.sqrt(math.pi)
CUTOFF_SQ = 144.0
KICK_SCALE = 0.04
CELL_WIDTH = 12.0
CELL_HEIGHT = 24.0

def atom_features(positions, charges, atom_type, patch_fill, sigma_table, eps_table):
    onehot = (atom_type[None] == jnp.arange(sigma_table.shape[0], dtype=jnp.int32)[:, None, None]).astype(jnp.float32)
    sigma = lax.optimization_barrier(jnp.sum(onehot * sigma_table[:, None, None], axis=0))
    depth = lax.optimization_barrier(jnp.sum(onehot * jnp.sqrt(eps_table)[:, None, None], axis=0))
    present = jnp.arange(charges.shape[1], dtype=jnp.int32)[None, :] < patch_fill[:, None]
    features = jnp.stack([positions[0], positions[1], positions[2], jnp.where(present, charges, 0.0), sigma, jnp.where(present, depth, 0.0)])
    return (features, onehot)

def cell_shift(first_patch, second_patch, patches, width_cells, layers):
    depth_cells = patches // width_cells
    first_within = first_patch % patches
    second_within = second_patch % patches
    step_x = (second_within % width_cells - first_within % width_cells + 1 + width_cells) % width_cells - 1
    step_y = (second_within // width_cells - first_within // width_cells + 1 + depth_cells) % depth_cells - 1
    step_z = (second_patch // patches - first_patch // patches + 1 + layers) % layers - 1
    return (CELL_WIDTH * step_x.astype(jnp.float32), CELL_WIDTH * step_y.astype(jnp.float32), CELL_HEIGHT * step_z.astype(jnp.float32))

def pair_block(first_atoms, second_atoms, shift, self_pair):
    delta_x = first_atoms[0][:, :, None] - second_atoms[0][:, None, :] - shift[0][:, None, None]
    delta_y = first_atoms[1][:, :, None] - second_atoms[1][:, None, :] - shift[1][:, None, None]
    delta_z = first_atoms[2][:, :, None] - second_atoms[2][:, None, :] - shift[2][:, None, None]
    dist_sq = delta_x * delta_x + delta_y * delta_y + delta_z * delta_z
    slots = jnp.arange(first_atoms.shape[2], dtype=jnp.int32)
    excluded = jnp.logical_and(self_pair[:, None, None], (slots[:, None] == slots[None, :])[None])
    dist_sq = jnp.where(excluded, 1.0, dist_sq)
    within = jnp.logical_and(dist_sq < CUTOFF_SQ, jnp.logical_not(excluded))
    inverse_sq = 1.0 / dist_sq
    distance = jnp.sqrt(dist_sq)
    sigma_pair = 0.5 * (first_atoms[4][:, :, None] + second_atoms[4][:, None, :])
    ratio_two = sigma_pair * sigma_pair * inverse_sq
    ratio_six = ratio_two * ratio_two * ratio_two
    depth_pair = first_atoms[5][:, :, None] * second_atoms[5][:, None, :]
    dispersion = 24.0 * depth_pair * (2.0 * ratio_six * ratio_six - ratio_six) * inverse_sq
    charge_pair = COULOMB * first_atoms[3][:, :, None] * second_atoms[3][:, None, :]
    screened = charge_pair * (jax.scipy.special.erfc(SPLIT_BETA * distance) / distance + GAUSS_FACTOR * jnp.exp(-SPLIT_BETA * SPLIT_BETA * dist_sq)) * inverse_sq
    magnitude = jnp.where(within, dispersion + screened, 0.0)
    pull_x = magnitude * delta_x
    pull_y = magnitude * delta_y
    pull_z = magnitude * delta_z
    on_first = jnp.stack([lax.optimization_barrier(jnp.sum(pull_x, axis=2)), lax.optimization_barrier(jnp.sum(pull_y, axis=2)), lax.optimization_barrier(jnp.sum(pull_z, axis=2))])
    on_second = -jnp.stack([lax.optimization_barrier(jnp.sum(pull_x, axis=1)), lax.optimization_barrier(jnp.sum(pull_y, axis=1)), lax.optimization_barrier(jnp.sum(pull_z, axis=1))])
    return (on_first, on_second)

def add_patch(totals, patch, term):
    current = lax.dynamic_slice_in_dim(totals, patch, 1, 1)
    return lax.dynamic_update_slice_in_dim(totals, current + term, patch, 1)

def reference(positions, velocities, charges, atom_type, patch_fill, sigma_table, eps_table, inv_mass_table, pair_first, pair_second):
    features, onehot = atom_features(positions, charges, atom_type, patch_fill, sigma_table, eps_table)
    firsts = pair_first.reshape(-1).astype(jnp.int32)
    raw_seconds = pair_second.reshape(-1).astype(jnp.int32)
    usable = raw_seconds >= 0
    seconds = jnp.where(usable, raw_seconds, firsts).astype(jnp.int32)

    def apply_slot(totals, slot):
        first_patch, second_patch, active = slot
        first_atoms = lax.dynamic_slice_in_dim(features, first_patch, 1, 1)
        second_atoms = lax.dynamic_slice_in_dim(features, second_patch, 1, 1)
        shift = cell_shift(first_patch[None], second_patch[None], P_DEV, PX, GROUPS)
        self_pair = (first_patch == second_patch)[None]
        on_first, on_second = pair_block(first_atoms, second_atoms, shift, self_pair)
        weight_first = jnp.where(active, 1.0, 0.0).astype(jnp.float32)
        weight_second = jnp.where(first_patch == second_patch, 0.0, weight_first).astype(jnp.float32)
        totals = add_patch(totals, first_patch, weight_first * on_first)
        totals = add_patch(totals, second_patch, weight_second * on_second)
        return (totals, None)
    zeros = jnp.zeros(positions.shape, jnp.float32)
    forces, unused = lax.scan(apply_slot, zeros, (firsts, seconds, usable))
    inverse_mass = lax.optimization_barrier(jnp.sum(onehot * inv_mass_table[:, None, None], axis=0))
    new_velocities = velocities + KICK_SCALE * inverse_mass[None] * forces
    new_positions = positions + new_velocities
    return (new_velocities, new_positions)
```

```python
import math

import jax
import jax.numpy as jnp
from jax import lax
from jax.experimental import pallas as pl
from jax.experimental.pallas import tpu as pltpu
from jax.sharding import PartitionSpec as P

PX = 8
EXT = 48
OWN = 32
SUBS = 4
VMEM_BYTES = 48 * 1024 * 1024
GROUP = 2
UNROLL = 4
COULOMB = 332.0636
SPLIT_BETA = 0.2
CUTOFF_SQ = 144.0
KICK_SCALE = 0.04
CELL_WIDTH = 12.0
CELL_HEIGHT = 24.0
STEP_W = SPLIT_BETA * CELL_WIDTH
STEP_H = SPLIT_BETA * CELL_HEIGHT
CUT = SPLIT_BETA * SPLIT_BETA * CUTOFF_SQ
GAUSS = 2.0 / math.sqrt(math.pi)
LOG2E = math.log2(math.e)
SIGMA_SCALE = SPLIT_BETA * 0.5 * 2.0 ** (1.0 / 6.0)
DEPTH_SCALE = math.sqrt(12.0 * SPLIT_BETA)
CHARGE_SCALE = math.sqrt(COULOMB * SPLIT_BETA * SPLIT_BETA)
FAR = 1.0e4
PARTS = 2
MESH = pl.DeviceIdType.MESH
F32 = jnp.float32
BF16 = jnp.bfloat16


def split3(value):
    high = value.astype(BF16)
    rest = value - high.astype(F32)
    mid = rest.astype(BF16)
    low = (rest - mid.astype(F32)).astype(BF16)
    return high, mid, low


def lookup(kind, table_ref, scale, root):
    value = jnp.zeros(kind.shape, F32)
    for t in range(8):
        value = jnp.where(kind == t, table_ref[0:1, t : t + 1], value)
    if root:
        value = jnp.sqrt(value)
    return value * scale


def prep_kernel(
    pos_ref,
    charge_ref,
    type_ref,
    fill_ref,
    sigma_ref,
    eps_ref,
    fj_ref,
    fu_ref,
    rank_ref,
    low_ref,
    feat_ref,
    place_ref,
    send_sem,
    recv_sem,
):
    group = lax.axis_index("patch")
    groups = lax.axis_size("patch")
    below = lax.rem(group + groups - 1, groups)
    above = lax.rem(group + 1, groups)
    barrier = pltpu.get_barrier_semaphore()
    pl.semaphore_signal(barrier, inc=1, device_id={"patch": above}, device_id_type=MESH)
    lane = lax.broadcasted_iota(jnp.int32, (128, 128), 1)
    row = lax.broadcasted_iota(jnp.int32, (128, 128), 0)
    fill = jnp.broadcast_to(fill_ref[0:1, :].astype(F32), (128, 128)).T
    present = lane.astype(F32) < fill
    kind = type_ref[...]
    z = pos_ref[2]
    feat_ref[0:128] = jnp.where(present, pos_ref[0] * SPLIT_BETA, -FAR)
    feat_ref[128:256] = pos_ref[1] * SPLIT_BETA
    feat_ref[256:384] = z * SPLIT_BETA
    feat_ref[384:512] = jnp.where(present, charge_ref[...] * CHARGE_SCALE, 0.0)
    feat_ref[512:640] = lookup(kind, sigma_ref, SIGMA_SCALE, False)
    feat_ref[640:768] = jnp.where(present, lookup(kind, eps_ref, DEPTH_SCALE, True), 0.0)
    feat_ref[768:896] = jnp.where(present, pos_ref[0] * SPLIT_BETA, FAR)
    feat_ref[896:1024] = jnp.zeros((128, 128), F32)
    low = jnp.logical_and(present, z < 0.5 * CELL_HEIGHT).astype(F32)
    high = jnp.logical_and(present, z >= 0.5 * CELL_HEIGHT).astype(F32)
    upto = (row <= lane).astype(F32).astype(BF16)
    low_upto = jnp.dot(low.astype(BF16), upto, preferred_element_type=F32)
    high_upto = jnp.dot(high.astype(BF16), upto, preferred_element_type=F32)
    low_count = jnp.sum(low, axis=1, keepdims=True)
    place_ref[...] = jnp.where(
        low > 0.0,
        low_upto - 1.0,
        jnp.where(high > 0.0, low_count + high_upto - 1.0, lane.astype(F32)),
    )
    counts = lax.dot_general(
        jnp.ones((8, 128), BF16), low.astype(BF16), (((1,), (1,)), ((), ())), preferred_element_type=F32
    )
    low_ref[...] = counts.astype(jnp.int32)
    first = lax.axis_index("sub") * OWN - PX + 128
    slot = row.astype(F32)

    def one(k, carry):
        p = (first + k) & 127
        place = place_ref[pl.ds(p, 1), :]
        rank_ref[pl.ds(k, 1), :] = place
        hit = (place == slot).astype(F32).astype(BF16)
        tile = feat_ref[pl.ds(p, 8, stride=128), :]
        total = jnp.zeros((8, 128), F32)
        for part in split3(tile):
            total = total + lax.dot_general(
                part, hit, (((1,), (1,)), ((), ())), preferred_element_type=F32
            )
        fj_ref[k] = total
        return carry

    pl.semaphore_wait(barrier, 1)
    copies = []
    for part in range(PARTS):
        size = EXT // PARTS
        lax.fori_loop(part * size, (part + 1) * size, one, 0, unroll=4)
        copy = pltpu.make_async_remote_copy(
            src_ref=fj_ref.at[pl.ds(part * size, size)],
            dst_ref=fu_ref.at[pl.ds(part * size, size)],
            send_sem=send_sem.at[part],
            recv_sem=recv_sem.at[part],
            device_id={"patch": below},
            device_id_type=MESH,
        )
        copy.start()
        copies.append(copy)
    for copy in copies:
        copy.wait()


def unit(lead, ref, b, own=None):
    xi, yi, zi, qi, si, ei = lead
    dx = xi - ref[b, 0:1, :]
    dy = yi - ref[b, 1:2, :]
    dz = zi - ref[b, 2:3, :]
    v = dx * dx + dy * dy + dz * dz
    if own is not None:
        v = jnp.where(own, 2.0 * CUT, v)
    w = lax.rsqrt(v)
    w2 = w * w
    u = (si + ref[b, 4:5, :]) * w
    u = u * u
    u = u * u * u
    screened = (1.0 - lax.erf(v * w)) * w + GAUSS * jnp.exp2(v * (-LOG2E))
    both = (ei * ref[b, 5:6, :]) * (u * u - u) + (qi * ref[b, 3:4, :]) * screened
    m = jnp.where(v < CUT, both * w2, 0.0)
    return m * dx, m * dy, m * dz


def pair_kernel(
    sub_ref, fill_ref, low_ref, fj_ref, fu_ref, own_ref, up_ref, lead_ref, blk_ref, a1_ref, acc_ref, accu_ref
):
    lane8 = lax.broadcasted_iota(jnp.int32, (8, 128), 1)
    row8 = lax.broadcasted_iota(jnp.int32, (8, 128), 0)
    half = lane8 < 64
    first = sub_ref[0] * OWN - PX + 128

    def clear(k, carry):
        acc_ref[k] = jnp.zeros((24, 128), F32)
        accu_ref[k] = jnp.zeros((24, 128), F32)
        return carry

    lax.fori_loop(0, EXT, clear, 0)
    own_ref[...] = jnp.zeros((3, EXT, 128), F32)

    def pack(p, worst):
        even = fu_ref[2 * p]
        odd = fu_ref[2 * p + 1]
        worst = jnp.maximum(worst, jnp.where(even[0:1] > -1.0, 0.5 * STEP_H - even[2:3], 0.0))
        worst = jnp.maximum(worst, jnp.where(odd[0:1] > -1.0, 0.5 * STEP_H - odd[2:3], 0.0))
        odd = jnp.where(row8 == 0, odd + STEP_W, odd)
        blk_ref[p] = jnp.where(half, even, pltpu.roll(odd, 64, 1))
        blk_ref[24 + p] = jnp.where(half, pltpu.roll(even, 64, 1), odd)
        return worst

    worst = lax.fori_loop(0, 24, pack, jnp.zeros((1, 128), F32))
    spill = jnp.max(jnp.where(lane8[0:1] >= 64, worst, 0.0)) > 0.0

    def lead_of(k, c):
        return tuple(lead_ref[k, f, pl.ds(c * 8, 8), :] for f in range(6))

    def add(total, term):
        return tuple(t + u for t, u in zip(total, term))

    def drain(ref, b, total):
        for d in range(3):
            ref[b, 8 * d : 8 * d + 8, :] -= total[d]

    def plane_units(ia, x, c, leads):
        left = ia - x + ((x + 7) & 7)
        right = ia - x + ((x + 1) & 7)
        force = [unit(lead, fj_ref, ia, (row8 + (c + n) * 8) == lane8) for n, lead in enumerate(leads)]
        for sx, sy, b in ((1, 0, right), (-1, 1, left + PX), (0, 1, ia + PX), (1, 1, right + PX)):
            total = None
            for n, (xi, yi, zi, qi, si, ei) in enumerate(leads):
                xs = xi - sx * STEP_W if sx else xi
                ys = yi - sy * STEP_W if sy else yi
                term = unit((xs, ys, zi, qi, si, ei), fj_ref, b)
                force[n] = add(force[n], term)
                total = term if total is None else add(total, term)
            drain(acc_ref, b, total)
        return force

    def up_units(ia, x, leads, base, force):
        shift = STEP_W * (x & 1).astype(F32)
        p1 = (x + 1) // 2
        p0 = (p1 + 3) & 3
        p1 = p1 & 3
        r = ia // PX
        for dr in (-1, 0, 1):
            for side, p in ((2.0 * STEP_W, p0), (0.0, p1)):
                b = base + (r + dr) * 4 + p
                total = None
                for n, (xi, yi, zi, qi, si, ei) in enumerate(leads):
                    term = unit((xi + (side - shift), yi - STEP_W * dr, zi - STEP_H, qi, si, ei), blk_ref, b)
                    force[n] = add(force[n], term)
                    total = term if total is None else add(total, term)
                drain(accu_ref, b, total)
        return force

    def put(k, c, force):
        for n, total in enumerate(force):
            for d in range(3):
                a1_ref[k, d, pl.ds((c + n) * 8, 8), :] = total[d]

    def spread(k, carry):
        turned = fj_ref[k + PX].T
        for f, column in enumerate((6, 1, 2, 3, 4, 5)):
            lead_ref[k, f] = jnp.broadcast_to(turned[:, column : column + 1], (128, 128))
        a1_ref[k] = jnp.zeros((3, 128, 128), F32)
        return carry

    lax.fori_loop(0, OWN, spread, 0, unroll=UNROLL)

    def one(k, carry):
        ia = k + PX
        x = k & 7
        p = (first + ia) & 127
        chunks = (fill_ref[p] + 7) // 8
        below = low_ref[0, p] // 8

        def lower(g, carry):
            c = g * GROUP
            leads = [lead_of(k, c + n) for n in range(GROUP)]
            put(k, c, plane_units(ia, x, c, leads))
            return carry

        def upper(g, carry):
            c = g * GROUP
            leads = [lead_of(k, c + n) for n in range(GROUP)]
            put(k, c, up_units(ia, x, leads, 0, plane_units(ia, x, c, leads)))
            return carry

        cut = below // GROUP
        end = (chunks + GROUP - 1) // GROUP
        lax.fori_loop(0, cut, lower, 0)
        lax.fori_loop(cut, end, upper, 0)

        @pl.when(spill)
        def _():
            def more(c, carry):
                force = [tuple(a1_ref[k, d, pl.ds(c * 8, 8), :] for d in range(3))]
                put(k, c, up_units(ia, x, [lead_of(k, c)], 24, force))
                return carry

            lax.fori_loop(below, chunks, more, 0)

        return carry

    lax.fori_loop(0, OWN, one, 0)

    def gather(k, carry):
        for d in range(3):
            own_ref[d, pl.ds(k + PX, 1), :] = jnp.sum(a1_ref[k, d].T, axis=0, keepdims=True)
        return carry

    lax.fori_loop(0, OWN, gather, 0, unroll=UNROLL)

    def fold(ref, k, d):
        return jnp.sum(ref[k, 8 * d : 8 * d + 8, :], axis=0, keepdims=True)

    def finish(p, carry):
        for d in range(3):
            own_ref[d, pl.ds(2 * p, 1), :] += fold(acc_ref, 2 * p, d)
            own_ref[d, pl.ds(2 * p + 1, 1), :] += fold(acc_ref, 2 * p + 1, d)
            a = fold(accu_ref, p, d)
            b = fold(accu_ref, 24 + p, d)
            up_ref[d, pl.ds(2 * p, 1), :] = jnp.where(half[0:1], a, pltpu.roll(b, 64, 1))
            up_ref[d, pl.ds(2 * p + 1, 1), :] = jnp.where(half[0:1], pltpu.roll(a, 64, 1), b)
        return carry

    lax.fori_loop(0, 24, finish, 0)


def kick_kernel(
    own_ref,
    up_ref,
    rank_ref,
    type_ref,
    mass_ref,
    vel_ref,
    pos_ref,
    new_vel_ref,
    new_pos_ref,
    came_ref,
    parts_ref,
    up_send,
    up_recv,
    part_send,
    part_recv,
):
    group = lax.axis_index("patch")
    groups = lax.axis_size("patch")
    below = lax.rem(group + groups - 1, groups)
    above = lax.rem(group + 1, groups)
    me = lax.axis_index("sub")
    barrier = pltpu.get_barrier_semaphore()
    pl.semaphore_signal(barrier, inc=1, device_id={"patch": below}, device_id_type=MESH)
    for step in range(1, SUBS):
        peer = lax.rem(me + step, SUBS)
        pl.semaphore_signal(barrier, inc=1, device_id={"sub": peer}, device_id_type=MESH)
    pl.semaphore_wait(barrier, SUBS)
    raised = pltpu.make_async_remote_copy(
        src_ref=up_ref,
        dst_ref=came_ref,
        send_sem=up_send,
        recv_sem=up_recv,
        device_id={"patch": above},
        device_id_type=MESH,
    )
    raised.start()
    slot = lax.broadcasted_iota(jnp.int32, (128, 128), 0).astype(F32)
    row8 = lax.broadcasted_iota(jnp.int32, (8, 128), 0)

    def unsorted(ref, k):
        hit = (rank_ref[pl.ds(k, 1), :] == slot).astype(F32).astype(BF16)
        tile = [ref[d, pl.ds(k, 1), :] for d in range(3)]
        tile = jnp.where(row8 == 0, tile[0], jnp.where(row8 == 1, tile[1], tile[2]))
        total = jnp.zeros((8, 128), F32)
        for part in split3(tile):
            total = total + jnp.dot(part, hit, preferred_element_type=F32)
        return total

    def mine(k, carry):
        total = unsorted(own_ref, k)
        for d in range(3):
            parts_ref[me, d, pl.ds(k, 1), :] = total[d : d + 1, :]
        return carry

    def theirs(k, carry):
        total = unsorted(came_ref, k)
        for d in range(3):
            parts_ref[me, d, pl.ds(k, 1), :] += total[d : d + 1, :]
        return carry

    lax.fori_loop(0, EXT, mine, 0, unroll=4)
    raised.wait()
    lax.fori_loop(0, EXT, theirs, 0, unroll=4)
    copies = []
    for step in range(1, SUBS):
        copy = pltpu.make_async_remote_copy(
            src_ref=parts_ref.at[me],
            dst_ref=parts_ref.at[me],
            send_sem=part_send.at[step - 1],
            recv_sem=part_recv.at[step - 1],
            device_id={"sub": lax.rem(me + step, SUBS)},
            device_id_type=MESH,
        )
        copy.start()
        copies.append(copy)
    kick = lookup(type_ref[...], mass_ref, KICK_SCALE, False)
    for copy in copies:
        copy.wait()
    for s in range(SUBS):
        for d in range(3):
            force = parts_ref[s, d, PX : PX + OWN, :]
            head = parts_ref[(s + SUBS - 1) % SUBS, d, PX + OWN : EXT, :]
            tail = parts_ref[(s + 1) % SUBS, d, 0:PX, :]
            force = jnp.concatenate([force[0:8] + head, force[8:24], force[24:32] + tail], axis=0)
            rows = slice(s * OWN, (s + 1) * OWN)
            velocity = vel_ref[d, rows, :] + kick[rows] * force
            new_vel_ref[d, rows, :] = velocity
            new_pos_ref[d, rows, :] = pos_ref[d, rows, :] + velocity


VM = pl.BlockSpec(memory_space=pltpu.VMEM)
SM = pl.BlockSpec(memory_space=pltpu.SMEM)


def shape(*dims, dtype=F32):
    return jax.ShapeDtypeStruct(dims, dtype)


def prep_call(positions, charges, atom_type, patch_fill, sigma_table, eps_table):
    return pl.pallas_call(
        prep_kernel,
        out_shape=(
            shape(EXT, 8, 128),
            shape(EXT, 8, 128),
            shape(EXT, 128),
            shape(8, 128, dtype=jnp.int32),
        ),
        in_specs=[VM] * 6,
        out_specs=(VM, VM, VM, VM),
        scratch_shapes=[
            pltpu.VMEM((1024, 128), F32),
            pltpu.VMEM((128, 128), F32),
            pltpu.SemaphoreType.DMA((PARTS,)),
            pltpu.SemaphoreType.DMA((PARTS,)),
        ],
        compiler_params=pltpu.CompilerParams(
            vmem_limit_bytes=VMEM_BYTES, collective_id=0, has_side_effects=True
        ),
    )(positions, charges, atom_type, patch_fill[None], sigma_table[None], eps_table[None])


def pair_call(sub, patch_fill, low, features, above):
    return pl.pallas_call(
        pair_kernel,
        out_shape=(shape(3, EXT, 128), shape(3, EXT, 128)),
        in_specs=[SM, SM, SM, VM, VM],
        out_specs=(VM, VM),
        scratch_shapes=[
            pltpu.VMEM((OWN, 6, 128, 128), F32),
            pltpu.VMEM((EXT, 8, 128), F32),
            pltpu.VMEM((OWN, 3, 128, 128), F32),
            pltpu.VMEM((EXT, 24, 128), F32),
            pltpu.VMEM((EXT, 24, 128), F32),
        ],
        compiler_params=pltpu.CompilerParams(vmem_limit_bytes=VMEM_BYTES),
    )(sub, patch_fill, low, features, above)


def kick_call(own, up, rank, atom_type, inv_mass_table, velocities, positions):
    return pl.pallas_call(
        kick_kernel,
        out_shape=(shape(3, 128, 128), shape(3, 128, 128)),
        in_specs=[VM] * 7,
        out_specs=(VM, VM),
        scratch_shapes=[
            pltpu.VMEM((3, EXT, 128), F32),
            pltpu.VMEM((SUBS, 3, EXT, 128), F32),
            pltpu.SemaphoreType.DMA,
            pltpu.SemaphoreType.DMA,
            pltpu.SemaphoreType.DMA((SUBS - 1,)),
            pltpu.SemaphoreType.DMA((SUBS - 1,)),
        ],
        compiler_params=pltpu.CompilerParams(
            vmem_limit_bytes=VMEM_BYTES, collective_id=1, has_side_effects=True
        ),
    )(own, up, rank, atom_type, inv_mass_table[None], velocities, positions)


def local(
    positions,
    velocities,
    charges,
    atom_type,
    patch_fill,
    sigma_table,
    eps_table,
    inv_mass_table,
    pair_first,
    pair_second,
):
    sub = lax.axis_index("sub").astype(jnp.int32).reshape(1)
    features, above, rank, low = prep_call(positions, charges, atom_type, patch_fill, sigma_table, eps_table)
    own, up = pair_call(sub, patch_fill, low, features, above)
    return kick_call(own, up, rank, atom_type, inv_mass_table, velocities, positions)


def solution(mesh):
    return jax.shard_map(
        local,
        mesh=mesh,
        in_specs=(
            P(None, "patch", None),
            P(None, "patch", None),
            P("patch", None),
            P("patch", None),
            P("patch"),
            P(),
            P(),
            P(),
            P("patch", "sub", None),
            P("patch", "sub", None),
        ),
        out_specs=(P(None, "patch", None), P(None, "patch", None)),
        check_vma=False,
    )
```

```python
import math

import jax
import jax.numpy as jnp
from jax import lax
from jax.experimental import pallas as pl
from jax.experimental.pallas import tpu as pltpu
from jax.sharding import PartitionSpec as P

PX = 8
EXT = 48
OWN = 32
SUBS = 4
VMEM_BYTES = 48 * 1024 * 1024
COULOMB = 332.0636
SPLIT_BETA = 0.2
CUTOFF_SQ = 144.0
KICK_SCALE = 0.04
CELL_WIDTH = 12.0
CELL_HEIGHT = 24.0
STEP_W = SPLIT_BETA * CELL_WIDTH
STEP_H = SPLIT_BETA * CELL_HEIGHT
CUT = SPLIT_BETA * SPLIT_BETA * CUTOFF_SQ
GAUSS = 2.0 / math.sqrt(math.pi)
LOG2E = math.log2(math.e)
SIGMA_SCALE = SPLIT_BETA * 0.5 * 2.0 ** (1.0 / 6.0)
DEPTH_SCALE = math.sqrt(12.0 * SPLIT_BETA)
CHARGE_SCALE = math.sqrt(COULOMB * SPLIT_BETA * SPLIT_BETA)
FAR = 1.0e4
FIRST = 16
SECOND = 24
MESH = pl.DeviceIdType.MESH
F32 = jnp.float32
BF16 = jnp.bfloat16


def stacked(tile):
    high = tile.astype(BF16).astype(F32)
    rest = tile - high
    mid = rest.astype(BF16).astype(F32)
    return jnp.concatenate([high, mid, rest - mid, jnp.zeros((8, 128), F32)], axis=0).astype(BF16)


def lookup(kind, table_ref, scale, root):
    value = jnp.zeros(kind.shape, F32)
    for t in range(8):
        value = jnp.where(kind == t, table_ref[0:1, t : t + 1], value)
    if root:
        value = jnp.sqrt(value)
    return value * scale


def first_kernel(
    pos_ref,
    charge_ref,
    type_ref,
    fill_ref,
    sigma_ref,
    eps_ref,
    fj_ref,
    fu_ref,
    rank_ref,
    own_ref,
    feat_ref,
    place_ref,
    lead0_ref,
    lead1_ref,
    sum0_ref,
    sum1_ref,
    acc_ref,
    send_sem,
    recv_sem,
):
    group = lax.axis_index("patch")
    groups = lax.axis_size("patch")
    below = lax.rem(group + groups - 1, groups)
    above = lax.rem(group + 1, groups)
    barrier = pltpu.get_barrier_semaphore()
    pl.semaphore_signal(barrier, inc=1, device_id={"patch": above}, device_id_type=MESH)
    lane = lax.broadcasted_iota(jnp.int32, (128, 128), 1)
    row = lax.broadcasted_iota(jnp.int32, (128, 128), 0)
    fill = jnp.broadcast_to(fill_ref[0:1, :].astype(F32), (128, 128)).T
    present = lane.astype(F32) < fill
    kind = type_ref[...]
    z = pos_ref[2]
    feat_ref[0:128] = jnp.where(present, pos_ref[0] * SPLIT_BETA, -FAR)
    feat_ref[128:256] = pos_ref[1] * SPLIT_BETA
    feat_ref[256:384] = z * SPLIT_BETA
    feat_ref[384:512] = jnp.where(present, charge_ref[...] * CHARGE_SCALE, 0.0)
    feat_ref[512:640] = lookup(kind, sigma_ref, SIGMA_SCALE, False)
    feat_ref[640:768] = jnp.where(present, lookup(kind, eps_ref, DEPTH_SCALE, True), 0.0)
    feat_ref[768:896] = kind.astype(F32)
    low = jnp.logical_and(present, z < 0.5 * CELL_HEIGHT).astype(F32)
    high = jnp.logical_and(present, z >= 0.5 * CELL_HEIGHT).astype(F32)
    upto = (row <= lane).astype(F32).astype(BF16)
    low_upto = jnp.dot(low.astype(BF16), upto, preferred_element_type=F32)
    high_upto = jnp.dot(high.astype(BF16), upto, preferred_element_type=F32)
    low_count = jnp.sum(low, axis=1, keepdims=True)
    high_count = jnp.sum(high, axis=1, keepdims=True)
    fits = jnp.logical_and(low_count <= 64.0, high_count <= 64.0)
    column = lane.astype(F32)
    gap = low_count + column - fill
    place_ref[...] = jnp.where(
        low > 0.0,
        low_upto - 1.0,
        jnp.where(
            high > 0.0,
            jnp.where(fits, 64.0, low_count) + high_upto - 1.0,
            jnp.where(jnp.logical_and(fits, gap < 64.0), gap, column),
        ),
    )
    feat_ref[896:1024] = jnp.broadcast_to(jnp.where(fits, 0.0, 1.0), (128, 128))
    first = lax.axis_index("sub") * OWN - PX + 128
    slot = row.astype(F32)

    def one(k, carry):
        p = (first + k) & 127
        place = place_ref[pl.ds(p, 1), :]
        rank_ref[pl.ds(k, 1), :] = place
        hit = (place == slot).astype(F32).astype(BF16)
        tile = feat_ref[pl.ds(p, 8, stride=128), :]
        total = lax.dot_general(stacked(tile), hit, (((1,), (1,)), ((), ())), preferred_element_type=F32)
        fj_ref[k] = total[0:8] + total[8:16] + total[16:24]
        return carry

    lax.fori_loop(0, EXT, one, 0, unroll=4)
    clear(acc_ref, own_ref)
    pl.semaphore_wait(barrier, 1)
    copy = pltpu.make_async_remote_copy(
        src_ref=fj_ref,
        dst_ref=fu_ref,
        send_sem=send_sem,
        recv_sem=recv_sem,
        device_id={"patch": below},
        device_id_type=MESH,
    )
    copy.start()
    plane_patches(0, FIRST, fj_ref, (lead0_ref, lead1_ref), (sum0_ref, sum1_ref), acc_ref, own_ref)
    add_folded(acc_ref, own_ref)
    copy.wait()


def spread(tile, lead_ref, rows):
    row8 = lax.broadcasted_iota(jnp.int32, (8, 128), 0)
    hidden = jnp.logical_and(row8 == 0, tile < -1.0)
    turned = jnp.where(hidden, FAR, tile).T
    for f in range(6):
        lead_ref[f] = jnp.broadcast_to(turned[128 - rows : 128, f : f + 1], (rows, 128))


def pair_block(lead_ref, cols, same):
    rows = lead_ref.shape[1]
    delta = [lead_ref[d] - cols[d : d + 1] for d in range(3)]
    v = delta[0] * delta[0] + delta[1] * delta[1] + delta[2] * delta[2]
    w = lax.rsqrt(v)
    w2 = w * w
    u = (lead_ref[4] + cols[4:5]) * w
    u = u * u
    u = u * u * u
    screened = (1.0 - lax.erf(v * w)) * w + GAUSS * jnp.exp2(v * (-LOG2E))
    both = (lead_ref[5] * cols[5:6]) * (u * u - u) + (lead_ref[3] * cols[3:4]) * screened
    keep = v < CUT
    if same:
        i = lax.broadcasted_iota(jnp.int32, (rows, 128), 0)
        j = lax.broadcasted_iota(jnp.int32, (rows, 128), 1)
        keep = jnp.logical_and(keep, i != j)
    force = jnp.where(keep, both * w2, 0.0)
    return [force * t for t in delta]


def fold8(value):
    total = value[0:8]
    for r in range(8, value.shape[0], 8):
        total = total + value[r : r + 8]
    return total


def moved(tile, x, y, z):
    row8 = lax.broadcasted_iota(jnp.int32, (8, 128), 0)
    return tile + jnp.where(row8 == 0, x, jnp.where(row8 == 1, y, jnp.where(row8 == 2, z, 0.0)))


def plane_patch(k, fj_ref, lead_ref, sum_ref, acc_ref):
    ia = k + PX
    x = k % PX
    left = ia - x + (x + PX - 1) % PX
    right = ia - x + (x + 1) % PX
    kinds = ((0, 0, ia), (1, 0, right), (-1, 1, left + PX), (0, 1, ia + PX), (1, 1, right + PX))
    for n, (sx, sy, b) in enumerate(kinds):
        pull = pair_block(lead_ref, moved(fj_ref[b], STEP_W * sx, STEP_W * sy, 0.0), n == 0)
        for d in range(3):
            if n == 0:
                sum_ref[d] = pull[d]
            else:
                sum_ref[d] += pull[d]
                acc_ref[b, 8 * d : 8 * d + 8, :] -= fold8(pull[d])


def plane_patches(start, stop, fj_ref, leads, sums, acc_ref, own_ref):
    def two(t, carry):
        k = start + 2 * t
        for n in range(2):
            plane_patch(k + n, fj_ref, leads[n], sums[n], acc_ref)
            spread(fj_ref[k + n + 2 + PX], leads[n], 128)
            for d in range(3):
                own_ref[d, pl.ds(k + n + PX, 1), :] = jnp.sum(sums[n][d].T, axis=0, keepdims=True)
        return carry

    spread(fj_ref[start + PX], leads[0], 128)
    spread(fj_ref[start + 1 + PX], leads[1], 128)
    lax.fori_loop(0, (stop - start) // 2, two, 0)


def clear(acc_ref, own_ref):
    def one(k, carry):
        acc_ref[k] = jnp.zeros((24, 128), F32)
        return carry

    lax.fori_loop(0, EXT, one, 0, unroll=4)
    own_ref[...] = jnp.zeros(own_ref.shape, F32)


def fold(ref, k, d):
    return jnp.sum(ref[k, 8 * d : 8 * d + 8, :], axis=0, keepdims=True)


def add_folded(acc_ref, own_ref):
    def one(k, carry):
        for d in range(3):
            own_ref[d, pl.ds(k, 1), :] += fold(acc_ref, k, d)
        return carry

    lax.fori_loop(PX, EXT, one, 0, unroll=4)


def up_kernel(
    fj_ref, fu_ref, up_ref, own_ref, turn_ref, lead0_ref, lead1_ref, sum0_ref, sum1_ref, acc_ref, accr_ref, full_ref, sumf_ref
):
    lane8 = lax.broadcasted_iota(jnp.int32, (8, 128), 1)
    row8 = lax.broadcasted_iota(jnp.int32, (8, 128), 0)
    half = lane8 < 64
    leads = (lead0_ref, lead1_ref)
    sums = (sum0_ref, sum1_ref)
    sides = [(dr, dx) for dr in (-1, 0, 1) for dx in (-1, 0, 1)]

    def start(p, worst):
        tile = fu_ref[p]
        turn_ref[p] = pltpu.roll(tile, 64, 1)
        acc_ref[p] = jnp.zeros((24, 128), F32)
        accr_ref[p] = jnp.zeros((24, 128), F32)
        return jnp.maximum(worst, jnp.maximum(tile[7:8], fj_ref[p, 7:8, :]))

    worst = lax.fori_loop(0, EXT, start, jnp.zeros((1, 128), F32), unroll=4)
    spill = jnp.max(worst) > 0.0

    def others(k):
        x = k % PX
        base = k + PX - x
        return [(base + PX * dr + (x + dx + PX) % PX, STEP_W * dx, STEP_W * dr) for dr, dx in sides]

    def finish(k, sum_ref, rows):
        for d in range(3):
            total = jnp.sum(sum_ref[d].T, axis=0, keepdims=True)
            if rows < 128:
                total = jnp.concatenate([jnp.zeros((1, 128 - rows), F32), total], axis=1)
            own_ref[d, pl.ds(k, 1), :] = total

    @pl.when(jnp.logical_not(spill))
    def _():
        def patch(k, lead_ref, sum_ref):
            near = others(k)
            for n in range(0, 9, 2):
                p, px, py = near[n]
                cols = moved(fu_ref[p], px, py, STEP_H)
                if n < 8:
                    r, rx, ry = near[n + 1]
                    cols = jnp.where(half, cols, moved(turn_ref[r], rx, ry, STEP_H))
                else:
                    cols = jnp.where(jnp.logical_or(half, row8 > 0), cols, -FAR)
                pull = pair_block(lead_ref, cols, False)
                for d in range(3):
                    if n == 0:
                        sum_ref[d] = pull[d]
                    else:
                        sum_ref[d] += pull[d]
                    back = fold8(pull[d])
                    acc_ref[p, 8 * d : 8 * d + 8, :] -= back
                    if n < 8:
                        accr_ref[r, 8 * d : 8 * d + 8, :] -= back

        def two(t, carry):
            k = 2 * t
            for n in range(2):
                patch(k + n, leads[n], sums[n])
                spread(fj_ref[k + n + 2 + PX], leads[n], 64)
                finish(k + n, sums[n], 64)
            return carry

        spread(fj_ref[PX], leads[0], 64)
        spread(fj_ref[PX + 1], leads[1], 64)
        lax.fori_loop(0, OWN // 2, two, 0)

    @pl.when(spill)
    def _():
        def one(k, carry):
            spread(fj_ref[k + PX], full_ref, 128)
            for n, (p, px, py) in enumerate(others(k)):
                pull = pair_block(full_ref, moved(fu_ref[p], px, py, STEP_H), False)
                for d in range(3):
                    if n == 0:
                        sumf_ref[d] = pull[d]
                    else:
                        sumf_ref[d] += pull[d]
                    acc_ref[p, 8 * d : 8 * d + 8, :] -= fold8(pull[d])
            finish(k, sumf_ref, 128)
            return carry

        lax.fori_loop(0, OWN, one, 0)

    @pl.when(jnp.logical_not(spill))
    def _():
        def one(p, carry):
            for d in range(3):
                total = fold(acc_ref, p, d) + pltpu.roll(fold(accr_ref, p, d), 64, 1)
                up_ref[d, pl.ds(p, 1), :] = jnp.where(half[0:1], total, 0.0)
            return carry

        lax.fori_loop(0, EXT, one, 0, unroll=4)

    @pl.when(spill)
    def _():
        def one(p, carry):
            for d in range(3):
                up_ref[d, pl.ds(p, 1), :] = fold(acc_ref, p, d)
            return carry

        lax.fori_loop(0, EXT, one, 0)


def kick_kernel(
    fj_ref,
    first_ref,
    rise_ref,
    up_ref,
    rank_ref,
    type_ref,
    mass_ref,
    vel_ref,
    pos_ref,
    new_vel_ref,
    new_pos_ref,
    own_ref,
    lead0_ref,
    lead1_ref,
    sum0_ref,
    sum1_ref,
    acc_ref,
    came_ref,
    parts_ref,
    up_send,
    up_recv,
    part_send,
    part_recv,
):
    group = lax.axis_index("patch")
    groups = lax.axis_size("patch")
    below = lax.rem(group + groups - 1, groups)
    above = lax.rem(group + 1, groups)
    me = lax.axis_index("sub")
    barrier = pltpu.get_barrier_semaphore()
    pl.semaphore_signal(barrier, inc=1, device_id={"patch": below}, device_id_type=MESH)
    for step in range(1, SUBS):
        peer = lax.rem(me + step, SUBS)
        pl.semaphore_signal(barrier, inc=1, device_id={"sub": peer}, device_id_type=MESH)
    clear(acc_ref, own_ref)
    work = (fj_ref, (lead0_ref, lead1_ref), (sum0_ref, sum1_ref), acc_ref, own_ref)
    plane_patches(FIRST, SECOND, *work)
    pl.semaphore_wait(barrier, SUBS)
    raised = pltpu.make_async_remote_copy(
        src_ref=up_ref,
        dst_ref=came_ref,
        send_sem=up_send,
        recv_sem=up_recv,
        device_id={"patch": above},
        device_id_type=MESH,
    )
    raised.start()
    plane_patches(SECOND, OWN, *work)
    add_folded(acc_ref, own_ref)
    for d in range(3):
        own_ref[d] += first_ref[d]
        own_ref[d, PX : PX + OWN, :] += rise_ref[d]
    slot = lax.broadcasted_iota(jnp.int32, (128, 128), 0).astype(F32)
    row8 = lax.broadcasted_iota(jnp.int32, (8, 128), 0)
    raised.wait()

    def unsort(k, carry):
        hit = (rank_ref[pl.ds(k, 1), :] == slot).astype(F32).astype(BF16)
        tile = [own_ref[d, pl.ds(k, 1), :] + came_ref[d, pl.ds(k, 1), :] for d in range(3)]
        tile = jnp.where(row8 == 0, tile[0], jnp.where(row8 == 1, tile[1], tile[2]))
        total = jnp.dot(stacked(tile), hit, preferred_element_type=F32)
        total = total[0:8] + total[8:16] + total[16:24]
        for d in range(3):
            parts_ref[me, d, pl.ds(k, 1), :] = total[d : d + 1, :]
        return carry

    lax.fori_loop(0, EXT, unsort, 0, unroll=4)
    copies = []
    for step in range(1, SUBS):
        copy = pltpu.make_async_remote_copy(
            src_ref=parts_ref.at[me],
            dst_ref=parts_ref.at[me],
            send_sem=part_send.at[step - 1],
            recv_sem=part_recv.at[step - 1],
            device_id={"sub": lax.rem(me + step, SUBS)},
            device_id_type=MESH,
        )
        copy.start()
        copies.append(copy)
    kick = lookup(type_ref[...], mass_ref, KICK_SCALE, False)
    for copy in copies:
        copy.wait()
    for s in range(SUBS):
        for d in range(3):
            force = parts_ref[s, d, PX : PX + OWN, :]
            head = parts_ref[(s + SUBS - 1) % SUBS, d, PX + OWN : EXT, :]
            tail = parts_ref[(s + 1) % SUBS, d, 0:PX, :]
            force = jnp.concatenate([force[0:8] + head, force[8:24], force[24:32] + tail], axis=0)
            rows = slice(s * OWN, (s + 1) * OWN)
            velocity = vel_ref[d, rows, :] + kick[rows] * force
            new_vel_ref[d, rows, :] = velocity
            new_pos_ref[d, rows, :] = pos_ref[d, rows, :] + velocity


VM = pl.BlockSpec(memory_space=pltpu.VMEM)


def shape(*dims, dtype=F32):
    return jax.ShapeDtypeStruct(dims, dtype)


def work_shapes(rows):
    lead = pltpu.VMEM((6, rows, 128), F32)
    total = pltpu.VMEM((3, rows, 128), F32)
    return [lead, lead, total, total, pltpu.VMEM((EXT, 24, 128), F32)]


def first_call(positions, charges, atom_type, patch_fill, sigma_table, eps_table):
    return pl.pallas_call(
        first_kernel,
        out_shape=(shape(EXT, 8, 128), shape(EXT, 8, 128), shape(EXT, 128), shape(3, EXT, 128)),
        in_specs=[VM] * 6,
        out_specs=(VM, VM, VM, VM),
        scratch_shapes=[pltpu.VMEM((1024, 128), F32), pltpu.VMEM((128, 128), F32)]
        + work_shapes(128)
        + [pltpu.SemaphoreType.DMA, pltpu.SemaphoreType.DMA],
        compiler_params=pltpu.CompilerParams(
            vmem_limit_bytes=VMEM_BYTES, collective_id=0, has_side_effects=True
        ),
    )(positions, charges, atom_type, patch_fill[None], sigma_table[None], eps_table[None])


def up_call(features, above):
    return pl.pallas_call(
        up_kernel,
        out_shape=(shape(3, EXT, 128), shape(3, OWN, 128)),
        in_specs=[VM] * 2,
        out_specs=(VM, VM),
        scratch_shapes=[pltpu.VMEM((EXT, 8, 128), F32)]
        + work_shapes(64)
        + [pltpu.VMEM((EXT, 24, 128), F32), pltpu.VMEM((6, 128, 128), F32), pltpu.VMEM((3, 128, 128), F32)],
        compiler_params=pltpu.CompilerParams(vmem_limit_bytes=VMEM_BYTES),
    )(features, above)


def kick_call(features, first, rise, up, rank, atom_type, inv_mass_table, velocities, positions):
    return pl.pallas_call(
        kick_kernel,
        out_shape=(shape(3, 128, 128), shape(3, 128, 128)),
        in_specs=[VM] * 9,
        out_specs=(VM, VM),
        scratch_shapes=[pltpu.VMEM((3, EXT, 128), F32)]
        + work_shapes(128)
        + [
            pltpu.VMEM((3, EXT, 128), F32),
            pltpu.VMEM((SUBS, 3, EXT, 128), F32),
            pltpu.SemaphoreType.DMA,
            pltpu.SemaphoreType.DMA,
            pltpu.SemaphoreType.DMA((SUBS - 1,)),
            pltpu.SemaphoreType.DMA((SUBS - 1,)),
        ],
        compiler_params=pltpu.CompilerParams(
            vmem_limit_bytes=VMEM_BYTES, collective_id=1, has_side_effects=True
        ),
    )(features, first, rise, up, rank, atom_type, inv_mass_table[None], velocities, positions)


def local(
    positions,
    velocities,
    charges,
    atom_type,
    patch_fill,
    sigma_table,
    eps_table,
    inv_mass_table,
    pair_first,
    pair_second,
):
    features, above, rank, first = first_call(
        positions, charges, atom_type, patch_fill, sigma_table, eps_table
    )
    up, rise = up_call(features, above)
    return kick_call(features, first, rise, up, rank, atom_type, inv_mass_table, velocities, positions)


def solution(mesh):
    return jax.shard_map(
        local,
        mesh=mesh,
        in_specs=(
            P(None, "patch", None),
            P(None, "patch", None),
            P("patch", None),
            P("patch", None),
            P("patch"),
            P(),
            P(),
            P(),
            P("patch", "sub", None),
            P("patch", "sub", None),
        ),
        out_specs=(P(None, "patch", None), P(None, "patch", None)),
        check_vma=False,
    )
```

```python
import math

import jax
import jax.numpy as jnp
from jax import lax
from jax.experimental import pallas as pl
from jax.experimental.pallas import tpu as pltpu
from jax.sharding import PartitionSpec as P

PX = 8
EXT = 48
OWN = 32
SUBS = 4
VMEM_BYTES = 48 * 1024 * 1024
COULOMB = 332.0636
SPLIT_BETA = 0.2
CUTOFF_SQ = 144.0
KICK_SCALE = 0.04
CELL_WIDTH = 12.0
CELL_HEIGHT = 24.0
STEP_W = SPLIT_BETA * CELL_WIDTH
STEP_H = SPLIT_BETA * CELL_HEIGHT
CUT = SPLIT_BETA * SPLIT_BETA * CUTOFF_SQ
GAUSS = 2.0 / math.sqrt(math.pi)
LOG2E = math.log2(math.e)
SIGMA_SCALE = SPLIT_BETA * 0.5 * 2.0 ** (1.0 / 6.0)
DEPTH_SCALE = math.sqrt(12.0 * SPLIT_BETA)
CHARGE_SCALE = math.sqrt(COULOMB * SPLIT_BETA * SPLIT_BETA)
FAR = 1.0e4
FIRST = 4
SECOND = 12
THIRD = 20
PIECES = 2
MESH = pl.DeviceIdType.MESH
F32 = jnp.float32
BF16 = jnp.bfloat16


def stacked(tile):
    high = tile.astype(BF16).astype(F32)
    rest = tile - high
    mid = rest.astype(BF16).astype(F32)
    return jnp.concatenate([high, mid, rest - mid, jnp.zeros((8, 128), F32)], axis=0).astype(BF16)


def lookup(kind, table_ref, scale, root):
    value = jnp.zeros(kind.shape, F32)
    for t in range(8):
        value = jnp.where(kind == t, table_ref[0:1, t : t + 1], value)
    if root:
        value = jnp.sqrt(value)
    return value * scale


def first_kernel(
    atom_hbm,
    fill_hbm,
    sigma_hbm,
    eps_hbm,
    mass_hbm,
    fj_ref,
    fu_ref,
    rank_ref,
    own_ref,
    kick_ref,
    feat_ref,
    place_ref,
    lead0_ref,
    lead1_ref,
    sum0_ref,
    sum1_ref,
    acc_ref,
    atom_ref,
    fill_ref,
    sigma_ref,
    eps_ref,
    mass_ref,
    load_sem,
    send_sem,
    recv_sem,
):
    loads = [
        pltpu.make_async_copy(source, target, load_sem.at[n])
        for n, (source, target) in enumerate(
            (
                (atom_hbm, atom_ref),
                (fill_hbm, fill_ref),
                (sigma_hbm, sigma_ref),
                (eps_hbm, eps_ref),
                (mass_hbm, mass_ref),
            )
        )
    ]
    for load in loads:
        load.start()
    group = lax.axis_index("patch")
    groups = lax.axis_size("patch")
    below = lax.rem(group + groups - 1, groups)
    above = lax.rem(group + 1, groups)
    barrier = pltpu.get_barrier_semaphore()
    pl.semaphore_signal(barrier, inc=1, device_id={"patch": above}, device_id_type=MESH)
    for load in loads:
        load.wait()
    lane = lax.broadcasted_iota(jnp.int32, (128, 128), 1)
    row = lax.broadcasted_iota(jnp.int32, (128, 128), 0)
    fill = jnp.broadcast_to(fill_ref[0:1, :].astype(F32), (128, 128)).T
    present = lane.astype(F32) < fill
    kind = atom_ref[4]
    z = atom_ref[2]
    feat_ref[0:128] = jnp.where(present, atom_ref[0] * SPLIT_BETA, -FAR)
    feat_ref[128:256] = atom_ref[1] * SPLIT_BETA
    feat_ref[256:384] = z * SPLIT_BETA
    feat_ref[384:512] = jnp.where(present, atom_ref[3] * CHARGE_SCALE, 0.0)
    feat_ref[512:640] = lookup(kind, sigma_ref, SIGMA_SCALE, False)
    feat_ref[640:768] = jnp.where(present, lookup(kind, eps_ref, DEPTH_SCALE, True), 0.0)
    feat_ref[768:896] = jnp.zeros((128, 128), F32)
    kick_ref[...] = lookup(kind, mass_ref, KICK_SCALE, False)
    low = jnp.logical_and(present, z < 0.5 * CELL_HEIGHT).astype(F32)
    high = jnp.logical_and(present, z >= 0.5 * CELL_HEIGHT).astype(F32)
    upto = (row <= lane).astype(F32).astype(BF16)
    low_upto = jnp.dot(low.astype(BF16), upto, preferred_element_type=F32)
    high_upto = jnp.dot(high.astype(BF16), upto, preferred_element_type=F32)
    low_count = jnp.sum(low, axis=1, keepdims=True)
    high_count = jnp.sum(high, axis=1, keepdims=True)
    fits = jnp.logical_and(low_count <= 64.0, high_count <= 64.0)
    column = lane.astype(F32)
    gap = low_count + column - fill
    place_ref[...] = jnp.where(
        low > 0.0,
        low_upto - 1.0,
        jnp.where(
            high > 0.0,
            jnp.where(fits, 64.0, low_count) + high_upto - 1.0,
            jnp.where(jnp.logical_and(fits, gap < 64.0), gap, column),
        ),
    )
    feat_ref[896:1024] = jnp.broadcast_to(jnp.where(fits, 0.0, 1.0), (128, 128))
    first = lax.axis_index("sub") * OWN - PX + 128
    slot = row.astype(F32)

    def one(k, carry):
        p = (first + k) & 127
        place = place_ref[pl.ds(p, 1), :]
        rank_ref[pl.ds(k, 1), :] = place
        hit = (place == slot).astype(F32).astype(BF16)
        tile = feat_ref[pl.ds(p, 8, stride=128), :]
        total = lax.dot_general(stacked(tile), hit, (((1,), (1,)), ((), ())), preferred_element_type=F32)
        fj_ref[k] = total[0:8] + total[8:16] + total[16:24]
        return carry

    lax.fori_loop(0, EXT, one, 0, unroll=4)
    clear(acc_ref, own_ref)
    work = (fj_ref, (lead0_ref, lead1_ref), (sum0_ref, sum1_ref), acc_ref, own_ref)
    if FIRST:
        plane_patches(0, FIRST, *work)
    pl.semaphore_wait(barrier, 1)
    copy = pltpu.make_async_remote_copy(
        src_ref=fj_ref,
        dst_ref=fu_ref,
        send_sem=send_sem,
        recv_sem=recv_sem,
        device_id={"patch": below},
        device_id_type=MESH,
    )
    copy.start()
    plane_patches(FIRST, SECOND, *work)
    add_folded(acc_ref, own_ref)
    copy.wait()


def spread(tile, lead_ref, rows):
    row8 = lax.broadcasted_iota(jnp.int32, (8, 128), 0)
    hidden = jnp.logical_and(row8 == 0, tile < -1.0)
    turned = jnp.where(hidden, FAR, tile).T
    for f in range(6):
        lead_ref[f] = jnp.broadcast_to(turned[128 - rows : 128, f : f + 1], (rows, 128))


def pair_block(lead_ref, cols, keep=None, rows=slice(None)):
    delta = [lead_ref[d, rows] - cols[d : d + 1] for d in range(3)]
    v = delta[0] * delta[0] + delta[1] * delta[1] + delta[2] * delta[2]
    w = lax.rsqrt(v)
    w2 = w * w
    u = (lead_ref[4, rows] + cols[4:5]) * w
    u = u * u
    u = u * u * u
    screened = (1.0 - lax.erf(v * w)) * w + GAUSS * jnp.exp2(v * (-LOG2E))
    both = (lead_ref[5, rows] * cols[5:6]) * (u * u - u) + (lead_ref[3, rows] * cols[3:4]) * screened
    near = v < CUT
    if keep is not None:
        near = jnp.logical_and(near, keep)
    force = jnp.where(near, both * w2, 0.0)
    return [force * t for t in delta]


def others_than(rows, start):
    i = lax.broadcasted_iota(jnp.int32, (rows, 128), 0) + start
    return i != lax.broadcasted_iota(jnp.int32, (rows, 128), 1)


def fold8(value):
    total = value[0:8]
    for r in range(8, value.shape[0], 8):
        total = total + value[r : r + 8]
    return total


def moved(tile, x, y, z):
    row8 = lax.broadcasted_iota(jnp.int32, (8, 128), 0)
    return tile + jnp.where(row8 == 0, x, jnp.where(row8 == 1, y, jnp.where(row8 == 2, z, 0.0)))


def plane_patch(k, fj_ref, lead_ref, sum_ref, acc_ref):
    ia = k + PX
    x = k % PX
    left = ia - x + (x + PX - 1) % PX
    right = ia - x + (x + 1) % PX
    for n, (sx, sy, b) in enumerate(((1, 0, right), (-1, 1, left + PX), (0, 1, ia + PX), (1, 1, right + PX))):
        pull = pair_block(lead_ref, moved(fj_ref[b], STEP_W * sx, STEP_W * sy, 0.0))
        for d in range(3):
            if n == 0:
                sum_ref[d] = pull[d]
            else:
                sum_ref[d] += pull[d]
            acc_ref[b, 8 * d : 8 * d + 8, :] -= fold8(pull[d])
    half = lax.broadcasted_iota(jnp.int32, (8, 128), 1) < 64
    pull = pair_block(lead_ref, fj_ref[ia], others_than(64, 0), slice(0, 64))
    for d in range(3):
        sum_ref[d, 0:64] += pull[d]
        acc_ref[ia, 8 * d : 8 * d + 8, :] -= jnp.where(half, 0.0, fold8(pull[d]))


def plane_patches(start, stop, fj_ref, leads, sums, acc_ref, own_ref):
    def two(t, carry):
        k = start + 2 * t
        for n in range(2):
            plane_patch(k + n, fj_ref, leads[n], sums[n], acc_ref)
            spread(fj_ref[k + n + 2 + PX], leads[n], 128)
            for d in range(3):
                own_ref[d, pl.ds(k + n + PX, 1), :] = jnp.sum(sums[n][d].T, axis=0, keepdims=True)
        return carry

    spread(fj_ref[start + PX], leads[0], 128)
    spread(fj_ref[start + 1 + PX], leads[1], 128)
    lax.fori_loop(0, (stop - start) // 2, two, 0)


def clear(acc_ref, own_ref):
    def one(k, carry):
        acc_ref[k] = jnp.zeros((24, 128), F32)
        return carry

    lax.fori_loop(0, EXT, one, 0, unroll=4)
    own_ref[...] = jnp.zeros(own_ref.shape, F32)


def fold(ref, k, d):
    return jnp.sum(ref[k, 8 * d : 8 * d + 8, :], axis=0, keepdims=True)


def add_folded(acc_ref, own_ref):
    def one(k, carry):
        for d in range(3):
            own_ref[d, pl.ds(k, 1), :] += fold(acc_ref, k, d)
        return carry

    lax.fori_loop(PX, EXT, one, 0, unroll=4)


def up_kernel(
    fj_ref, fu_ref, up_ref, own_ref, turn_ref, lead0_ref, lead1_ref, sum0_ref, sum1_ref, acc_ref, accr_ref, full_ref, sumf_ref
):
    lane8 = lax.broadcasted_iota(jnp.int32, (8, 128), 1)
    row8 = lax.broadcasted_iota(jnp.int32, (8, 128), 0)
    half = lane8 < 64
    leads = (lead0_ref, lead1_ref)
    sums = (sum0_ref, sum1_ref)
    sides = [(dr, dx) for dr in (-1, 0, 1) for dx in (-1, 0, 1)]

    def start(p, worst):
        tile = fu_ref[p]
        turn_ref[p] = pltpu.roll(tile, 64, 1)
        acc_ref[p] = jnp.zeros((24, 128), F32)
        accr_ref[p] = jnp.zeros((24, 128), F32)
        return jnp.maximum(worst, jnp.maximum(tile[7:8], fj_ref[p, 7:8, :]))

    worst = lax.fori_loop(0, EXT, start, jnp.zeros((1, 128), F32), unroll=4)
    spill = jnp.max(worst) > 0.0

    def others(k):
        x = k % PX
        base = k + PX - x
        return [(base + PX * dr + (x + dx + PX) % PX, STEP_W * dx, STEP_W * dr) for dr, dx in sides]

    def finish(k, sum_ref, rows):
        for d in range(3):
            total = jnp.sum(sum_ref[d].T, axis=0, keepdims=True)
            if rows < 128:
                total = jnp.concatenate([jnp.zeros((1, 128 - rows), F32), total], axis=1)
            own_ref[d, pl.ds(k, 1), :] = total

    @pl.when(jnp.logical_not(spill))
    def _():
        def patch(k, lead_ref, sum_ref):
            near = others(k)
            for n in range(0, 9, 2):
                p, px, py = near[n]
                cols = moved(fu_ref[p], px, py, STEP_H)
                if n < 8:
                    r, rx, ry = near[n + 1]
                    cols = jnp.where(half, cols, moved(turn_ref[r], rx, ry, STEP_H))
                else:
                    cols = jnp.where(half, cols, fj_ref[k + PX])
                pull = pair_block(lead_ref, cols, others_than(64, 64) if n == 8 else None)
                for d in range(3):
                    if n == 0:
                        sum_ref[d] = pull[d]
                    else:
                        sum_ref[d] += pull[d]
                    back = fold8(pull[d])
                    acc_ref[p, 8 * d : 8 * d + 8, :] -= back
                    if n < 8:
                        accr_ref[r, 8 * d : 8 * d + 8, :] -= back

        def two(t, carry):
            k = 2 * t
            spread(fj_ref[k + 1 + PX], leads[1], 64)
            finish((k + OWN - 1) % OWN, sums[1], 64)
            patch(k, leads[0], sums[0])
            spread(fj_ref[k + 2 + PX], leads[0], 64)
            finish(k, sums[0], 64)
            patch(k + 1, leads[1], sums[1])
            return carry

        spread(fj_ref[PX], leads[0], 64)
        sum1_ref[...] = jnp.zeros(sum1_ref.shape, F32)
        lax.fori_loop(0, OWN // 2, two, 0)
        finish(OWN - 1, sums[1], 64)

    @pl.when(spill)
    def _():
        def one(k, carry):
            spread(fj_ref[k + PX], full_ref, 128)
            cols = jnp.where(jnp.logical_and(half, row8 == 0), -FAR, fj_ref[k + PX])
            for n, (p, px, py) in enumerate(others(k)):
                pull = pair_block(full_ref, moved(fu_ref[p], px, py, STEP_H))
                for d in range(3):
                    if n == 0:
                        sumf_ref[d] = pull[d]
                    else:
                        sumf_ref[d] += pull[d]
                    acc_ref[p, 8 * d : 8 * d + 8, :] -= fold8(pull[d])
            pull = pair_block(full_ref, cols, others_than(64, 64), slice(64, 128))
            for d in range(3):
                sumf_ref[d, 64:128] += pull[d]
            finish(k, sumf_ref, 128)
            return carry

        lax.fori_loop(0, OWN, one, 0)

    @pl.when(jnp.logical_not(spill))
    def _():
        def one(p, carry):
            for d in range(3):
                rows = slice(8 * d, 8 * d + 8)
                total = acc_ref[p, rows, :] + pltpu.roll(accr_ref[p, rows, :], 64, 1)
                total = jnp.sum(jnp.where(half, total, 0.0), axis=0, keepdims=True)
                up_ref[d, pl.ds(p, 1), :] = total
            return carry

        lax.fori_loop(0, EXT, one, 0, unroll=4)

    @pl.when(spill)
    def _():
        def one(p, carry):
            for d in range(3):
                up_ref[d, pl.ds(p, 1), :] = fold(acc_ref, p, d)
            return carry

        lax.fori_loop(0, EXT, one, 0)


def last_kernel(
    fj_ref,
    first_ref,
    rise_ref,
    up_ref,
    rank_ref,
    force_ref,
    own_ref,
    lead0_ref,
    lead1_ref,
    sum0_ref,
    sum1_ref,
    acc_ref,
    came_ref,
    parts_ref,
    up_send,
    up_recv,
    part_send,
    part_recv,
):
    group = lax.axis_index("patch")
    groups = lax.axis_size("patch")
    below = lax.rem(group + groups - 1, groups)
    above = lax.rem(group + 1, groups)
    me = lax.axis_index("sub")
    barrier = pltpu.get_barrier_semaphore()
    pl.semaphore_signal(barrier, inc=1, device_id={"patch": below}, device_id_type=MESH)
    for step in range(1, SUBS):
        peer = lax.rem(me + step, SUBS)
        pl.semaphore_signal(barrier, inc=1, device_id={"sub": peer}, device_id_type=MESH)
    clear(acc_ref, own_ref)
    work = (fj_ref, (lead0_ref, lead1_ref), (sum0_ref, sum1_ref), acc_ref, own_ref)
    plane_patches(SECOND, THIRD, *work)
    pl.semaphore_wait(barrier, SUBS)
    raised = pltpu.make_async_remote_copy(
        src_ref=up_ref,
        dst_ref=came_ref,
        send_sem=up_send,
        recv_sem=up_recv,
        device_id={"patch": above},
        device_id_type=MESH,
    )
    raised.start()
    plane_patches(THIRD, OWN, *work)
    add_folded(acc_ref, own_ref)
    for d in range(3):
        own_ref[d] += first_ref[d]
        own_ref[d, PX : PX + OWN, :] += rise_ref[d]
    slot = lax.broadcasted_iota(jnp.int32, (128, 128), 0).astype(F32)
    row8 = lax.broadcasted_iota(jnp.int32, (8, 128), 0)
    raised.wait()

    def unsort(k, carry):
        hit = (rank_ref[pl.ds(k, 1), :] == slot).astype(F32).astype(BF16)
        tile = [own_ref[d, pl.ds(k, 1), :] + came_ref[d, pl.ds(k, 1), :] for d in range(3)]
        tile = jnp.where(row8 == 0, tile[0], jnp.where(row8 == 1, tile[1], tile[2]))
        total = jnp.dot(stacked(tile), hit, preferred_element_type=F32)
        total = total[0:8] + total[8:16] + total[16:24]
        for d in range(3):
            parts_ref[me, d, pl.ds(k, 1), :] = total[d : d + 1, :]
        return carry

    copies = []
    for piece in range(PIECES):
        rows = pl.ds(piece * (EXT // PIECES), EXT // PIECES)
        lax.fori_loop(piece * (EXT // PIECES), (piece + 1) * (EXT // PIECES), unsort, 0, unroll=4)
        for step in range(1, SUBS):
            copy = pltpu.make_async_remote_copy(
                src_ref=parts_ref.at[me, :, rows],
                dst_ref=parts_ref.at[me, :, rows],
                send_sem=part_send.at[piece, step - 1],
                recv_sem=part_recv.at[piece, step - 1],
                device_id={"sub": lax.rem(me + step, SUBS)},
                device_id_type=MESH,
            )
            copy.start()
            copies.append(copy)
    for copy in copies:
        copy.wait()
    for s in range(SUBS):
        for d in range(3):
            force = parts_ref[s, d, PX : PX + OWN, :]
            head = parts_ref[(s + SUBS - 1) % SUBS, d, PX + OWN : EXT, :]
            tail = parts_ref[(s + 1) % SUBS, d, 0:PX, :]
            force = jnp.concatenate([force[0:8] + head, force[8:24], force[24:32] + tail], axis=0)
            force_ref[d, s * OWN : (s + 1) * OWN, :] = force


VM = pl.BlockSpec(memory_space=pltpu.VMEM)


def shape(*dims, dtype=F32):
    return jax.ShapeDtypeStruct(dims, dtype)


def work_shapes(rows):
    lead = pltpu.VMEM((6, rows, 128), F32)
    total = pltpu.VMEM((3, rows, 128), F32)
    return [lead, lead, total, total, pltpu.VMEM((EXT, 24, 128), F32)]


def first_call(atoms, patch_fill, *tables):
    return pl.pallas_call(
        first_kernel,
        out_shape=(
            shape(EXT, 8, 128),
            shape(EXT, 8, 128),
            shape(EXT, 128),
            shape(3, EXT, 128),
            shape(128, 128),
        ),
        in_specs=[pl.BlockSpec(memory_space=pltpu.HBM)] * 5,
        out_specs=(VM,) * 5,
        scratch_shapes=[pltpu.VMEM((1024, 128), F32), pltpu.VMEM((128, 128), F32)]
        + work_shapes(128)
        + [
            pltpu.VMEM((5, 128, 128), F32),
            pltpu.VMEM((1, 128), jnp.int32),
            pltpu.VMEM((1, 8), F32),
            pltpu.VMEM((1, 8), F32),
            pltpu.VMEM((1, 8), F32),
            pltpu.SemaphoreType.DMA((5,)),
            pltpu.SemaphoreType.DMA,
            pltpu.SemaphoreType.DMA,
        ],
        compiler_params=pltpu.CompilerParams(
            vmem_limit_bytes=VMEM_BYTES, collective_id=0, has_side_effects=True
        ),
    )(atoms, patch_fill[None], *(table[None] for table in tables))


def up_call(features, above):
    return pl.pallas_call(
        up_kernel,
        out_shape=(shape(3, EXT, 128), shape(3, OWN, 128)),
        in_specs=[VM] * 2,
        out_specs=(VM, VM),
        scratch_shapes=[pltpu.VMEM((EXT, 8, 128), F32)]
        + work_shapes(64)
        + [pltpu.VMEM((EXT, 24, 128), F32), pltpu.VMEM((6, 128, 128), F32), pltpu.VMEM((3, 128, 128), F32)],
        compiler_params=pltpu.CompilerParams(vmem_limit_bytes=VMEM_BYTES),
    )(features, above)


def last_call(features, first, rise, up, rank):
    return pl.pallas_call(
        last_kernel,
        out_shape=shape(3, 128, 128),
        in_specs=[VM] * 5,
        out_specs=VM,
        scratch_shapes=[pltpu.VMEM((3, EXT, 128), F32)]
        + work_shapes(128)
        + [
            pltpu.VMEM((3, EXT, 128), F32),
            pltpu.VMEM((SUBS, 3, EXT, 128), F32),
            pltpu.SemaphoreType.DMA,
            pltpu.SemaphoreType.DMA,
            pltpu.SemaphoreType.DMA((PIECES, SUBS - 1)),
            pltpu.SemaphoreType.DMA((PIECES, SUBS - 1)),
        ],
        compiler_params=pltpu.CompilerParams(
            vmem_limit_bytes=VMEM_BYTES, collective_id=1, has_side_effects=True
        ),
    )(features, first, rise, up, rank)


def local(
    positions,
    velocities,
    charges,
    atom_type,
    patch_fill,
    sigma_table,
    eps_table,
    inv_mass_table,
    pair_first,
    pair_second,
):
    atoms = jnp.concatenate([positions, charges[None], atom_type.astype(F32)[None]])
    features, above, rank, first, kick = first_call(
        atoms, patch_fill, sigma_table, eps_table, inv_mass_table
    )
    up, rise = up_call(features, above)
    forces = last_call(features, first, rise, up, rank)
    new_velocities = velocities + kick[None] * forces
    new_positions = positions + new_velocities
    return (new_velocities, new_positions)


def solution(mesh):
    return jax.shard_map(
        local,
        mesh=mesh,
        in_specs=(
            P(None, "patch", None),
            P(None, "patch", None),
            P("patch", None),
            P("patch", None),
            P("patch"),
            P(),
            P(),
            P(),
            P("patch", "sub", None),
            P("patch", "sub", None),
        ),
        out_specs=(P(None, "patch", None), P(None, "patch", None)),
        check_vma=False,
    )
```

```python
import math

import jax
import jax.numpy as jnp
from jax import lax
from jax.experimental import pallas as pl
from jax.experimental.pallas import tpu as pltpu
from jax.sharding import PartitionSpec as P

PX = 8
EXT = 48
OWN = 32
SUBS = 4
VMEM_BYTES = 48 * 1024 * 1024
COULOMB = 332.0636
SPLIT_BETA = 0.2
CUTOFF_SQ = 144.0
KICK_SCALE = 0.04
CELL_WIDTH = 12.0
CELL_HEIGHT = 24.0
STEP_W = SPLIT_BETA * CELL_WIDTH
STEP_H = SPLIT_BETA * CELL_HEIGHT
CUT = SPLIT_BETA * SPLIT_BETA * CUTOFF_SQ
GAUSS = 2.0 / math.sqrt(math.pi)
LOG2E = math.log2(math.e)
SIGMA_SCALE = SPLIT_BETA * 0.5 * 2.0 ** (1.0 / 6.0)
DEPTH_SCALE = math.sqrt(12.0 * SPLIT_BETA)
CHARGE_SCALE = math.sqrt(COULOMB * SPLIT_BETA * SPLIT_BETA)
FAR = 1.0e4
FIRST = 6
SECOND = 12
THIRD = 20
PIECES = 3
MESH = pl.DeviceIdType.MESH
F32 = jnp.float32
BF16 = jnp.bfloat16


def stacked(tile):
    high = tile.astype(BF16).astype(F32)
    rest = tile - high
    mid = rest.astype(BF16).astype(F32)
    return jnp.concatenate([high, mid, rest - mid, jnp.zeros((8, 128), F32)], axis=0).astype(BF16)


def lookup(kind, table_ref, scale, root):
    value = jnp.zeros(kind.shape, F32)
    for t in range(8):
        value = jnp.where(kind == t, table_ref[0:1, t : t + 1], value)
    if root:
        value = jnp.sqrt(value)
    return value * scale


def first_kernel(
    atom_hbm,
    fill_hbm,
    sigma_hbm,
    eps_hbm,
    mass_hbm,
    fj_ref,
    fu_ref,
    rank_ref,
    own_ref,
    kick_ref,
    feat_ref,
    place_ref,
    lead0_ref,
    lead1_ref,
    sum0_ref,
    sum1_ref,
    acc_ref,
    atom_ref,
    fill_ref,
    sigma_ref,
    eps_ref,
    mass_ref,
    load_sem,
    send_sem,
    recv_sem,
):
    loads = [
        pltpu.make_async_copy(source, target, load_sem.at[n])
        for n, (source, target) in enumerate(
            (
                (atom_hbm, atom_ref),
                (fill_hbm, fill_ref),
                (sigma_hbm, sigma_ref),
                (eps_hbm, eps_ref),
                (mass_hbm, mass_ref),
            )
        )
    ]
    for load in loads:
        load.start()
    group = lax.axis_index("patch")
    groups = lax.axis_size("patch")
    below = lax.rem(group + groups - 1, groups)
    above = lax.rem(group + 1, groups)
    barrier = pltpu.get_barrier_semaphore()
    pl.semaphore_signal(barrier, inc=1, device_id={"patch": above}, device_id_type=MESH)
    for load in loads:
        load.wait()
    lane = lax.broadcasted_iota(jnp.int32, (128, 128), 1)
    row = lax.broadcasted_iota(jnp.int32, (128, 128), 0)
    fill = jnp.broadcast_to(fill_ref[0:1, :].astype(F32), (128, 128)).T
    present = lane.astype(F32) < fill
    kind = atom_ref[4]
    z = atom_ref[2]
    feat_ref[0:128] = jnp.where(present, atom_ref[0] * SPLIT_BETA, -FAR)
    feat_ref[128:256] = atom_ref[1] * SPLIT_BETA
    feat_ref[256:384] = z * SPLIT_BETA
    feat_ref[384:512] = jnp.where(present, atom_ref[3] * CHARGE_SCALE, 0.0)
    feat_ref[512:640] = lookup(kind, sigma_ref, SIGMA_SCALE, False)
    feat_ref[640:768] = jnp.where(present, lookup(kind, eps_ref, DEPTH_SCALE, True), 0.0)
    feat_ref[768:896] = jnp.zeros((128, 128), F32)
    kick_ref[...] = lookup(kind, mass_ref, KICK_SCALE, False)
    low = jnp.logical_and(present, z < 0.5 * CELL_HEIGHT).astype(F32)
    high = jnp.logical_and(present, z >= 0.5 * CELL_HEIGHT).astype(F32)
    upto = (row <= lane).astype(F32).astype(BF16)
    low_upto = jnp.dot(low.astype(BF16), upto, preferred_element_type=F32)
    high_upto = jnp.dot(high.astype(BF16), upto, preferred_element_type=F32)
    low_count = jnp.sum(low, axis=1, keepdims=True)
    high_count = jnp.sum(high, axis=1, keepdims=True)
    fits = jnp.logical_and(low_count <= 64.0, high_count <= 64.0)
    column = lane.astype(F32)
    gap = low_count + column - fill
    place_ref[...] = jnp.where(
        low > 0.0,
        low_upto - 1.0,
        jnp.where(
            high > 0.0,
            jnp.where(fits, 64.0, low_count) + high_upto - 1.0,
            jnp.where(jnp.logical_and(fits, gap < 64.0), gap, column),
        ),
    )
    feat_ref[896:1024] = jnp.broadcast_to(jnp.where(fits, 0.0, 1.0), (128, 128))
    first = lax.axis_index("sub") * OWN - PX + 128
    slot = row.astype(F32)

    def one(k, carry):
        p = (first + k) & 127
        place = place_ref[pl.ds(p, 1), :]
        rank_ref[pl.ds(k, 1), :] = place
        hit = (place == slot).astype(F32).astype(BF16)
        tile = feat_ref[pl.ds(p, 8, stride=128), :]
        total = lax.dot_general(stacked(tile), hit, (((1,), (1,)), ((), ())), preferred_element_type=F32)
        fj_ref[k] = total[0:8] + total[8:16] + total[16:24]
        return carry

    lax.fori_loop(0, EXT, one, 0, unroll=16)
    clear(acc_ref, own_ref)
    work = (fj_ref, (lead0_ref, lead1_ref), (sum0_ref, sum1_ref), acc_ref, own_ref)
    if FIRST:
        plane_patches(0, FIRST, *work)
    pl.semaphore_wait(barrier, 1)
    copy = pltpu.make_async_remote_copy(
        src_ref=fj_ref,
        dst_ref=fu_ref,
        send_sem=send_sem,
        recv_sem=recv_sem,
        device_id={"patch": below},
        device_id_type=MESH,
    )
    copy.start()
    plane_patches(FIRST, SECOND, *work)
    add_folded(acc_ref, own_ref)
    copy.wait()


def spread(tile, lead_ref, rows):
    row8 = lax.broadcasted_iota(jnp.int32, (8, 128), 0)
    hidden = jnp.logical_and(row8 == 0, tile < -1.0)
    turned = jnp.where(hidden, FAR, tile).T
    for f in range(6):
        lead_ref[f] = jnp.broadcast_to(turned[128 - rows : 128, f : f + 1], (rows, 128))


def pair_block(lead_ref, cols, keep=None, rows=slice(None)):
    delta = [lead_ref[d, rows] - cols[d : d + 1] for d in range(3)]
    v = delta[0] * delta[0] + delta[1] * delta[1] + delta[2] * delta[2]
    w = lax.rsqrt(v)
    w2 = w * w
    u = (lead_ref[4, rows] + cols[4:5]) * w
    u = u * u
    u = u * u * u
    screened = (1.0 - lax.erf(v * w)) * w + GAUSS * jnp.exp2(v * (-LOG2E))
    both = (lead_ref[5, rows] * cols[5:6]) * (u * u - u) + (lead_ref[3, rows] * cols[3:4]) * screened
    near = v < CUT
    if keep is not None:
        near = jnp.logical_and(near, keep)
    force = jnp.where(near, both * w2, 0.0)
    return [force * t for t in delta]


def others_than(rows, start):
    i = lax.broadcasted_iota(jnp.int32, (rows, 128), 0) + start
    return i != lax.broadcasted_iota(jnp.int32, (rows, 128), 1)


def fold8(value):
    total = value[0:8]
    for r in range(8, value.shape[0], 8):
        total = total + value[r : r + 8]
    return total


def moved(tile, x, y, z):
    row8 = lax.broadcasted_iota(jnp.int32, (8, 128), 0)
    return tile + jnp.where(row8 == 0, x, jnp.where(row8 == 1, y, jnp.where(row8 == 2, z, 0.0)))


def plane_patch(k, fj_ref, lead_ref, sum_ref, acc_ref):
    ia = k + PX
    x = k % PX
    left = ia - x + (x + PX - 1) % PX
    right = ia - x + (x + 1) % PX
    for n, (sx, sy, b) in enumerate(((1, 0, right), (-1, 1, left + PX), (0, 1, ia + PX), (1, 1, right + PX))):
        pull = pair_block(lead_ref, moved(fj_ref[b], STEP_W * sx, STEP_W * sy, 0.0))
        for d in range(3):
            if n == 0:
                sum_ref[d] = pull[d]
            else:
                sum_ref[d] += pull[d]
            acc_ref[b, 8 * d : 8 * d + 8, :] -= fold8(pull[d])
    half = lax.broadcasted_iota(jnp.int32, (8, 128), 1) < 64
    pull = pair_block(lead_ref, fj_ref[ia], others_than(64, 0), slice(0, 64))
    for d in range(3):
        sum_ref[d, 0:64] += pull[d]
        acc_ref[ia, 8 * d : 8 * d + 8, :] -= jnp.where(half, 0.0, fold8(pull[d]))


def plane_patches(start, stop, fj_ref, leads, sums, acc_ref, own_ref):
    def two(t, carry):
        k = start + 2 * t
        plane_patch(k, fj_ref, leads[0], sums[0], acc_ref)
        spread(fj_ref[k + 2 + PX], leads[0], 128)
        plane_patch(k + 1, fj_ref, leads[1], sums[1], acc_ref)
        for d in range(3):
            own_ref[d, pl.ds(k + PX, 1), :] = jnp.sum(sums[0][d].T, axis=0, keepdims=True)
        spread(fj_ref[k + 3 + PX], leads[1], 128)
        for d in range(3):
            own_ref[d, pl.ds(k + 1 + PX, 1), :] = jnp.sum(sums[1][d].T, axis=0, keepdims=True)
        return carry

    spread(fj_ref[start + PX], leads[0], 128)
    spread(fj_ref[start + 1 + PX], leads[1], 128)
    lax.fori_loop(0, (stop - start) // 2, two, 0)


def clear(acc_ref, own_ref):
    def one(k, carry):
        acc_ref[k] = jnp.zeros((24, 128), F32)
        return carry

    lax.fori_loop(0, EXT, one, 0, unroll=16)
    own_ref[...] = jnp.zeros(own_ref.shape, F32)


def fold(ref, k, d):
    return jnp.sum(ref[k, 8 * d : 8 * d + 8, :], axis=0, keepdims=True)


def add_folded(acc_ref, own_ref):
    def one(k, carry):
        for d in range(3):
            own_ref[d, pl.ds(k, 1), :] += fold(acc_ref, k, d)
        return carry

    lax.fori_loop(PX, EXT, one, 0, unroll=8)


def up_kernel(
    fj_ref, fu_ref, up_ref, own_ref, turn_ref, lead0_ref, lead1_ref, sum0_ref, sum1_ref, acc_ref, accr_ref, full_ref, sumf_ref
):
    lane8 = lax.broadcasted_iota(jnp.int32, (8, 128), 1)
    row8 = lax.broadcasted_iota(jnp.int32, (8, 128), 0)
    half = lane8 < 64
    leads = (lead0_ref, lead1_ref)
    sides = [(dr, dx) for dr in (-1, 0, 1) for dx in (-1, 0, 1)]

    def start(p, worst):
        tile = fu_ref[p]
        turn_ref[p] = pltpu.roll(tile, 64, 1)
        acc_ref[p] = jnp.zeros((24, 128), F32)
        accr_ref[p] = jnp.zeros((24, 128), F32)
        return jnp.maximum(worst, jnp.maximum(tile[7:8], fj_ref[p, 7:8, :]))

    worst = lax.fori_loop(0, EXT, start, jnp.zeros((1, 128), F32), unroll=8)
    spill = jnp.max(worst) > 0.0

    def others(k):
        x = k % PX
        base = k + PX - x
        return [(base + PX * dr + (x + dx + PX) % PX, STEP_W * dx, STEP_W * dr) for dr, dx in sides]

    def finish(k, sum_ref, rows):
        for d in range(3):
            total = jnp.sum(sum_ref[d].T, axis=0, keepdims=True)
            if rows < 128:
                total = jnp.concatenate([jnp.zeros((1, 128 - rows), F32), total], axis=1)
            own_ref[d, pl.ds(k, 1), :] = total

    @pl.when(jnp.logical_not(spill))
    def _():
        def patch(k, lead_ref, rows):
            near = others(k)
            for n in range(0, 9, 2):
                p, px, py = near[n]
                cols = moved(fu_ref[p], px, py, STEP_H)
                if n < 8:
                    r, rx, ry = near[n + 1]
                    cols = jnp.where(half, cols, moved(turn_ref[r], rx, ry, STEP_H))
                else:
                    cols = jnp.where(half, cols, fj_ref[k + PX])
                pull = pair_block(lead_ref, cols, others_than(64, 64) if n == 8 else None)
                for d in range(3):
                    if n == 0:
                        sumf_ref[d, rows] = pull[d]
                    else:
                        sumf_ref[d, rows] += pull[d]
                    back = fold8(pull[d])
                    acc_ref[p, 8 * d : 8 * d + 8, :] -= back
                    if n < 8:
                        accr_ref[r, 8 * d : 8 * d + 8, :] -= back

        def finish_two(k):
            for d in range(3):
                total = jnp.sum(sumf_ref[d].T, axis=0, keepdims=True)
                own_ref[d, pl.ds(k, 1), :] = jnp.where(half[0:1], 0.0, pltpu.roll(total, 64, 1))
                own_ref[d, pl.ds(k + 1, 1), :] = jnp.where(half[0:1], 0.0, total)

        def two(t, carry):
            k = 2 * t
            spread(fj_ref[k + 1 + PX], leads[1], 64)
            finish_two((k + OWN - 2) % OWN)
            patch(k, leads[0], slice(0, 64))
            spread(fj_ref[k + 2 + PX], leads[0], 64)
            patch(k + 1, leads[1], slice(64, 128))
            return carry

        spread(fj_ref[PX], leads[0], 64)
        sumf_ref[...] = jnp.zeros(sumf_ref.shape, F32)
        lax.fori_loop(0, OWN // 2, two, 0)
        finish_two(OWN - 2)

    @pl.when(spill)
    def _():
        def one(k, carry):
            spread(fj_ref[k + PX], full_ref, 128)
            cols = jnp.where(jnp.logical_and(half, row8 == 0), -FAR, fj_ref[k + PX])
            for n, (p, px, py) in enumerate(others(k)):
                pull = pair_block(full_ref, moved(fu_ref[p], px, py, STEP_H))
                for d in range(3):
                    if n == 0:
                        sumf_ref[d] = pull[d]
                    else:
                        sumf_ref[d] += pull[d]
                    acc_ref[p, 8 * d : 8 * d + 8, :] -= fold8(pull[d])
            pull = pair_block(full_ref, cols, others_than(64, 64), slice(64, 128))
            for d in range(3):
                sumf_ref[d, 64:128] += pull[d]
            finish(k, sumf_ref, 128)
            return carry

        lax.fori_loop(0, OWN, one, 0)

    @pl.when(jnp.logical_not(spill))
    def _():
        def one(p, carry):
            for d in range(3):
                rows = slice(8 * d, 8 * d + 8)
                total = acc_ref[p, rows, :] + pltpu.roll(accr_ref[p, rows, :], 64, 1)
                total = jnp.sum(jnp.where(half, total, 0.0), axis=0, keepdims=True)
                up_ref[d, pl.ds(p, 1), :] = total
            return carry

        lax.fori_loop(0, EXT, one, 0, unroll=16)

    @pl.when(spill)
    def _():
        def one(p, carry):
            for d in range(3):
                up_ref[d, pl.ds(p, 1), :] = fold(acc_ref, p, d)
            return carry

        lax.fori_loop(0, EXT, one, 0)


def last_kernel(
    fj_ref,
    first_ref,
    rise_ref,
    up_ref,
    rank_ref,
    force_ref,
    own_ref,
    lead0_ref,
    lead1_ref,
    sum0_ref,
    sum1_ref,
    acc_ref,
    came_ref,
    parts_ref,
    up_send,
    up_recv,
    part_send,
    part_recv,
):
    group = lax.axis_index("patch")
    groups = lax.axis_size("patch")
    below = lax.rem(group + groups - 1, groups)
    above = lax.rem(group + 1, groups)
    me = lax.axis_index("sub")
    barrier = pltpu.get_barrier_semaphore()
    pl.semaphore_signal(barrier, inc=1, device_id={"patch": below}, device_id_type=MESH)
    for step in range(1, SUBS):
        peer = lax.rem(me + step, SUBS)
        pl.semaphore_signal(barrier, inc=1, device_id={"sub": peer}, device_id_type=MESH)
    clear(acc_ref, own_ref)
    work = (fj_ref, (lead0_ref, lead1_ref), (sum0_ref, sum1_ref), acc_ref, own_ref)
    plane_patches(SECOND, THIRD, *work)
    pl.semaphore_wait(barrier, SUBS)
    raised = pltpu.make_async_remote_copy(
        src_ref=up_ref,
        dst_ref=came_ref,
        send_sem=up_send,
        recv_sem=up_recv,
        device_id={"patch": above},
        device_id_type=MESH,
    )
    raised.start()
    plane_patches(THIRD, OWN, *work)
    add_folded(acc_ref, own_ref)
    for d in range(3):
        own_ref[d] += first_ref[d]
        own_ref[d, PX : PX + OWN, :] += rise_ref[d]
    slot = lax.broadcasted_iota(jnp.int32, (128, 128), 0).astype(F32)
    row8 = lax.broadcasted_iota(jnp.int32, (8, 128), 0)
    raised.wait()

    def unsort(k, carry):
        hit = (rank_ref[pl.ds(k, 1), :] == slot).astype(F32).astype(BF16)
        tile = [own_ref[d, pl.ds(k, 1), :] + came_ref[d, pl.ds(k, 1), :] for d in range(3)]
        tile = jnp.where(row8 == 0, tile[0], jnp.where(row8 == 1, tile[1], tile[2]))
        total = jnp.dot(stacked(tile), hit, preferred_element_type=F32)
        total = total[0:8] + total[8:16] + total[16:24]
        for d in range(3):
            parts_ref[me, d, pl.ds(k, 1), :] = total[d : d + 1, :]
        return carry

    copies = []
    for piece in range(PIECES):
        rows = pl.ds(piece * (EXT // PIECES), EXT // PIECES)
        lax.fori_loop(piece * (EXT // PIECES), (piece + 1) * (EXT // PIECES), unsort, 0, unroll=16)
        for step in range(1, SUBS):
            copy = pltpu.make_async_remote_copy(
                src_ref=parts_ref.at[me, :, rows],
                dst_ref=parts_ref.at[me, :, rows],
                send_sem=part_send.at[piece, step - 1],
                recv_sem=part_recv.at[piece, step - 1],
                device_id={"sub": lax.rem(me + step, SUBS)},
                device_id_type=MESH,
            )
            copy.start()
            copies.append(copy)
    for copy in copies:
        copy.wait()
    for s in range(SUBS):
        for d in range(3):
            force = parts_ref[s, d, PX : PX + OWN, :]
            head = parts_ref[(s + SUBS - 1) % SUBS, d, PX + OWN : EXT, :]
            tail = parts_ref[(s + 1) % SUBS, d, 0:PX, :]
            force = jnp.concatenate([force[0:8] + head, force[8:24], force[24:32] + tail], axis=0)
            force_ref[d, s * OWN : (s + 1) * OWN, :] = force


VM = pl.BlockSpec(memory_space=pltpu.VMEM)


def shape(*dims, dtype=F32):
    return jax.ShapeDtypeStruct(dims, dtype)


def work_shapes(rows):
    lead = pltpu.VMEM((6, rows, 128), F32)
    total = pltpu.VMEM((3, rows, 128), F32)
    return [lead, lead, total, total, pltpu.VMEM((EXT, 24, 128), F32)]


def first_call(atoms, patch_fill, *tables):
    return pl.pallas_call(
        first_kernel,
        out_shape=(
            shape(EXT, 8, 128),
            shape(EXT, 8, 128),
            shape(EXT, 128),
            shape(3, EXT, 128),
            shape(128, 128),
        ),
        in_specs=[pl.BlockSpec(memory_space=pltpu.HBM)] * 5,
        out_specs=(VM,) * 5,
        scratch_shapes=[pltpu.VMEM((1024, 128), F32), pltpu.VMEM((128, 128), F32)]
        + work_shapes(128)
        + [
            pltpu.VMEM((5, 128, 128), F32),
            pltpu.VMEM((1, 128), jnp.int32),
            pltpu.VMEM((1, 8), F32),
            pltpu.VMEM((1, 8), F32),
            pltpu.VMEM((1, 8), F32),
            pltpu.SemaphoreType.DMA((5,)),
            pltpu.SemaphoreType.DMA,
            pltpu.SemaphoreType.DMA,
        ],
        compiler_params=pltpu.CompilerParams(
            vmem_limit_bytes=VMEM_BYTES, collective_id=0, has_side_effects=True
        ),
    )(atoms, patch_fill[None], *(table[None] for table in tables))


def up_call(features, above):
    return pl.pallas_call(
        up_kernel,
        out_shape=(shape(3, EXT, 128), shape(3, OWN, 128)),
        in_specs=[VM] * 2,
        out_specs=(VM, VM),
        scratch_shapes=[pltpu.VMEM((EXT, 8, 128), F32)]
        + work_shapes(64)
        + [pltpu.VMEM((EXT, 24, 128), F32), pltpu.VMEM((6, 128, 128), F32), pltpu.VMEM((3, 128, 128), F32)],
        compiler_params=pltpu.CompilerParams(vmem_limit_bytes=VMEM_BYTES),
    )(features, above)


def last_call(features, first, rise, up, rank):
    return pl.pallas_call(
        last_kernel,
        out_shape=shape(3, 128, 128),
        in_specs=[VM] * 5,
        out_specs=VM,
        scratch_shapes=[pltpu.VMEM((3, EXT, 128), F32)]
        + work_shapes(128)
        + [
            pltpu.VMEM((3, EXT, 128), F32),
            pltpu.VMEM((SUBS, 3, EXT, 128), F32),
            pltpu.SemaphoreType.DMA,
            pltpu.SemaphoreType.DMA,
            pltpu.SemaphoreType.DMA((PIECES, SUBS - 1)),
            pltpu.SemaphoreType.DMA((PIECES, SUBS - 1)),
        ],
        compiler_params=pltpu.CompilerParams(
            vmem_limit_bytes=VMEM_BYTES, collective_id=1, has_side_effects=True
        ),
    )(features, first, rise, up, rank)


def local(
    positions,
    velocities,
    charges,
    atom_type,
    patch_fill,
    sigma_table,
    eps_table,
    inv_mass_table,
    pair_first,
    pair_second,
):
    plane = lax.broadcasted_iota(jnp.int32, (5, 128, 128), 0)
    atoms = jnp.where(plane == 3, charges[None], atom_type.astype(F32)[None])
    atoms = jnp.where(plane < 3, jnp.pad(positions, ((0, 2), (0, 0), (0, 0))), atoms)
    features, above, rank, first, kick = first_call(
        atoms, patch_fill, sigma_table, eps_table, inv_mass_table
    )
    up, rise = up_call(features, above)
    forces = last_call(features, first, rise, up, rank)
    new_velocities = velocities + kick[None] * forces
    new_positions = positions + new_velocities
    return (new_velocities, new_positions)


def solution(mesh):
    return jax.shard_map(
        local,
        mesh=mesh,
        in_specs=(
            P(None, "patch", None),
            P(None, "patch", None),
            P("patch", None),
            P("patch", None),
            P("patch"),
            P(),
            P(),
            P(),
            P("patch", "sub", None),
            P("patch", "sub", None),
        ),
        out_specs=(P(None, "patch", None), P(None, "patch", None)),
        check_vma=False,
    )
```

```python
import math

import jax
import jax.numpy as jnp
from jax import lax
from jax.experimental import pallas as pl
from jax.experimental.pallas import tpu as pltpu
from jax.sharding import PartitionSpec as P

PX = 8
EXT = 48
OWN = 32
SUBS = 4
VMEM_BYTES = 48 * 1024 * 1024
COULOMB = 332.0636
SPLIT_BETA = 0.2
CUTOFF_SQ = 144.0
KICK_SCALE = 0.04
CELL_WIDTH = 12.0
CELL_HEIGHT = 24.0
STEP_W = SPLIT_BETA * CELL_WIDTH
STEP_H = SPLIT_BETA * CELL_HEIGHT
CUT = SPLIT_BETA * SPLIT_BETA * CUTOFF_SQ
GAUSS = 2.0 / math.sqrt(math.pi)
LOG2E = math.log2(math.e)
SIGMA_SCALE = SPLIT_BETA * 0.5 * 2.0 ** (1.0 / 6.0)
DEPTH_SCALE = math.sqrt(12.0 * SPLIT_BETA)
CHARGE_SCALE = math.sqrt(COULOMB * SPLIT_BETA * SPLIT_BETA)
FAR = 1.0e4
FIRST = 6
SECOND = 12
THIRD = 20
PIECES = 3
MESH = pl.DeviceIdType.MESH
F32 = jnp.float32
BF16 = jnp.bfloat16


def stacked(tile):
    high = tile.astype(BF16).astype(F32)
    rest = tile - high
    mid = rest.astype(BF16).astype(F32)
    return jnp.concatenate([high, mid, rest - mid, jnp.zeros((8, 128), F32)], axis=0).astype(BF16)


def lookup(kind, table_ref, scale, root):
    value = jnp.zeros(kind.shape, F32)
    for t in range(8):
        value = jnp.where(kind == t, table_ref[0:1, t : t + 1], value)
    if root:
        value = jnp.sqrt(value)
    return value * scale


def first_kernel(
    atom_hbm,
    fill_hbm,
    sigma_hbm,
    eps_hbm,
    mass_hbm,
    fj_ref,
    fu_ref,
    rank_ref,
    own_ref,
    kick_ref,
    feat_ref,
    place_ref,
    lead0_ref,
    lead1_ref,
    sum0_ref,
    sum1_ref,
    acc_ref,
    atom_ref,
    fill_ref,
    sigma_ref,
    eps_ref,
    mass_ref,
    load_sem,
    send_sem,
    recv_sem,
):
    loads = [
        pltpu.make_async_copy(source, target, load_sem.at[n])
        for n, (source, target) in enumerate(
            (
                (atom_hbm, atom_ref),
                (fill_hbm, fill_ref),
                (sigma_hbm, sigma_ref),
                (eps_hbm, eps_ref),
                (mass_hbm, mass_ref),
            )
        )
    ]
    for load in loads:
        load.start()
    group = lax.axis_index("patch")
    groups = lax.axis_size("patch")
    below = lax.rem(group + groups - 1, groups)
    above = lax.rem(group + 1, groups)
    barrier = pltpu.get_barrier_semaphore()
    pl.semaphore_signal(barrier, inc=1, device_id={"patch": above}, device_id_type=MESH)
    for load in loads:
        load.wait()
    lane = lax.broadcasted_iota(jnp.int32, (128, 128), 1)
    row = lax.broadcasted_iota(jnp.int32, (128, 128), 0)
    fill = jnp.broadcast_to(fill_ref[0:1, :].astype(F32), (128, 128)).T
    present = lane.astype(F32) < fill
    kind = atom_ref[4]
    z = atom_ref[2]
    feat_ref[0:128] = jnp.where(present, atom_ref[0] * SPLIT_BETA, -FAR)
    feat_ref[128:256] = atom_ref[1] * SPLIT_BETA
    feat_ref[256:384] = z * SPLIT_BETA
    feat_ref[384:512] = jnp.where(present, atom_ref[3] * CHARGE_SCALE, 0.0)
    feat_ref[512:640] = lookup(kind, sigma_ref, SIGMA_SCALE, False)
    feat_ref[640:768] = jnp.where(present, lookup(kind, eps_ref, DEPTH_SCALE, True), 0.0)
    feat_ref[768:896] = jnp.zeros((128, 128), F32)
    kick_ref[...] = lookup(kind, mass_ref, KICK_SCALE, False)
    low = jnp.logical_and(present, z < 0.5 * CELL_HEIGHT).astype(F32)
    high = jnp.logical_and(present, z >= 0.5 * CELL_HEIGHT).astype(F32)
    upto = (row <= lane).astype(F32).astype(BF16)
    low_upto = jnp.dot(low.astype(BF16), upto, preferred_element_type=F32)
    high_upto = jnp.dot(high.astype(BF16), upto, preferred_element_type=F32)
    low_count = jnp.sum(low, axis=1, keepdims=True)
    high_count = jnp.sum(high, axis=1, keepdims=True)
    fits = jnp.logical_and(low_count <= 64.0, high_count <= 64.0)
    column = lane.astype(F32)
    gap = low_count + column - fill
    place_ref[...] = jnp.where(
        low > 0.0,
        low_upto - 1.0,
        jnp.where(
            high > 0.0,
            jnp.where(fits, 64.0, low_count) + high_upto - 1.0,
            jnp.where(jnp.logical_and(fits, gap < 64.0), gap, column),
        ),
    )
    feat_ref[896:1024] = jnp.broadcast_to(jnp.where(fits, 0.0, 1.0), (128, 128))
    first = lax.axis_index("sub") * OWN - PX + 128
    slot = row.astype(F32)

    def one(k, carry):
        p = (first + k) & 127
        place = place_ref[pl.ds(p, 1), :]
        rank_ref[pl.ds(k, 1), :] = place
        hit = (place == slot).astype(F32).astype(BF16)
        tile = feat_ref[pl.ds(p, 8, stride=128), :]
        total = lax.dot_general(stacked(tile), hit, (((1,), (1,)), ((), ())), preferred_element_type=F32)
        fj_ref[k] = total[0:8] + total[8:16] + total[16:24]
        return carry

    lax.fori_loop(0, EXT, one, 0, unroll=16)
    clear(acc_ref, own_ref)
    work = (fj_ref, (lead0_ref, lead1_ref), (sum0_ref, sum1_ref), acc_ref, own_ref)
    if FIRST:
        plane_patches(0, FIRST, *work)
    pl.semaphore_wait(barrier, 1)
    copy = pltpu.make_async_remote_copy(
        src_ref=fj_ref,
        dst_ref=fu_ref,
        send_sem=send_sem,
        recv_sem=recv_sem,
        device_id={"patch": below},
        device_id_type=MESH,
    )
    copy.start()
    plane_patches(FIRST, SECOND, *work)
    add_folded(acc_ref, own_ref)
    copy.wait()


def spread(tile, lead_ref, rows):
    row8 = lax.broadcasted_iota(jnp.int32, (8, 128), 0)
    hidden = jnp.logical_and(row8 == 0, tile < -1.0)
    turned = jnp.where(hidden, FAR, tile).T
    for f in range(6):
        lead_ref[f] = jnp.broadcast_to(turned[128 - rows : 128, f : f + 1], (rows, 128))


def pair_block(lead_ref, cols, keep=None, rows=slice(None)):
    delta = [lead_ref[d, rows] - cols[d : d + 1] for d in range(3)]
    v = delta[0] * delta[0] + delta[1] * delta[1] + delta[2] * delta[2]
    w = lax.rsqrt(v)
    w2 = w * w
    u = (lead_ref[4, rows] + cols[4:5]) * w
    u = u * u
    u = u * u * u
    screened = (1.0 - lax.erf(v * w)) * w + GAUSS * jnp.exp2(v * (-LOG2E))
    both = (lead_ref[5, rows] * cols[5:6]) * (u * u - u) + (lead_ref[3, rows] * cols[3:4]) * screened
    near = v < CUT
    if keep is not None:
        near = jnp.logical_and(near, keep)
    force = jnp.where(near, both * w2, 0.0)
    return [force * t for t in delta]


def others_than(rows, start):
    i = lax.broadcasted_iota(jnp.int32, (rows, 128), 0) + start
    return i != lax.broadcasted_iota(jnp.int32, (rows, 128), 1)


def fold8(value):
    total = value[0:8]
    for r in range(8, value.shape[0], 8):
        total = total + value[r : r + 8]
    return total


def moved(tile, x, y, z):
    row8 = lax.broadcasted_iota(jnp.int32, (8, 128), 0)
    return tile + jnp.where(row8 == 0, x, jnp.where(row8 == 1, y, jnp.where(row8 == 2, z, 0.0)))


def plane_patch(k, fj_ref, lead_ref, sum_ref, acc_ref):
    ia = k + PX
    x = k % PX
    left = ia - x + (x + PX - 1) % PX
    right = ia - x + (x + 1) % PX
    for n, (sx, sy, b) in enumerate(((1, 0, right), (-1, 1, left + PX), (0, 1, ia + PX), (1, 1, right + PX))):
        pull = pair_block(lead_ref, moved(fj_ref[b], STEP_W * sx, STEP_W * sy, 0.0))
        for d in range(3):
            if n == 0:
                sum_ref[d] = pull[d]
            else:
                sum_ref[d] += pull[d]
            acc_ref[b, 8 * d : 8 * d + 8, :] -= fold8(pull[d])
    half = lax.broadcasted_iota(jnp.int32, (8, 128), 1) < 64
    pull = pair_block(lead_ref, fj_ref[ia], others_than(64, 0), slice(0, 64))
    for d in range(3):
        sum_ref[d, 0:64] += pull[d]
        acc_ref[ia, 8 * d : 8 * d + 8, :] -= jnp.where(half, 0.0, fold8(pull[d]))


def plane_patches(start, stop, fj_ref, leads, sums, acc_ref, own_ref):
    def two(t, carry):
        k = start + 2 * t
        plane_patch(k, fj_ref, leads[0], sums[0], acc_ref)
        spread(fj_ref[k + 2 + PX], leads[0], 128)
        plane_patch(k + 1, fj_ref, leads[1], sums[1], acc_ref)
        for d in range(3):
            own_ref[d, pl.ds(k + PX, 1), :] = jnp.sum(sums[0][d].T, axis=0, keepdims=True)
        spread(fj_ref[k + 3 + PX], leads[1], 128)
        for d in range(3):
            own_ref[d, pl.ds(k + 1 + PX, 1), :] = jnp.sum(sums[1][d].T, axis=0, keepdims=True)
        return carry

    spread(fj_ref[start + PX], leads[0], 128)
    spread(fj_ref[start + 1 + PX], leads[1], 128)
    lax.fori_loop(0, (stop - start) // 2, two, 0)


def clear(acc_ref, own_ref):
    def one(k, carry):
        acc_ref[k] = jnp.zeros((24, 128), F32)
        return carry

    lax.fori_loop(0, EXT, one, 0, unroll=16)
    own_ref[...] = jnp.zeros(own_ref.shape, F32)


def fold(ref, k, d):
    return jnp.sum(ref[k, 8 * d : 8 * d + 8, :], axis=0, keepdims=True)


def add_folded(acc_ref, own_ref):
    def one(k, carry):
        for d in range(3):
            own_ref[d, pl.ds(k, 1), :] += fold(acc_ref, k, d)
        return carry

    lax.fori_loop(PX, EXT, one, 0, unroll=20)


def up_kernel(
    fj_ref, fu_ref, up_ref, own_ref, turn_ref, lead0_ref, lead1_ref, sum0_ref, sum1_ref, acc_ref, accr_ref, full_ref, sumf_ref
):
    lane8 = lax.broadcasted_iota(jnp.int32, (8, 128), 1)
    row8 = lax.broadcasted_iota(jnp.int32, (8, 128), 0)
    half = lane8 < 64
    leads = (lead0_ref, lead1_ref)
    sides = [(dr, dx) for dr in (-1, 0, 1) for dx in (-1, 0, 1)]

    def start(p, worst):
        tile = fu_ref[p]
        turn_ref[p] = pltpu.roll(tile, 64, 1)
        acc_ref[p] = jnp.zeros((24, 128), F32)
        accr_ref[p] = jnp.zeros((24, 128), F32)
        return jnp.maximum(worst, jnp.maximum(tile[7:8], fj_ref[p, 7:8, :]))

    worst = lax.fori_loop(0, EXT, start, jnp.zeros((1, 128), F32), unroll=16)
    spill = jnp.max(worst) > 0.0

    def others(k):
        x = k % PX
        base = k + PX - x
        return [(base + PX * dr + (x + dx + PX) % PX, STEP_W * dx, STEP_W * dr) for dr, dx in sides]

    def finish(k, sum_ref, rows):
        for d in range(3):
            total = jnp.sum(sum_ref[d].T, axis=0, keepdims=True)
            if rows < 128:
                total = jnp.concatenate([jnp.zeros((1, 128 - rows), F32), total], axis=1)
            own_ref[d, pl.ds(k, 1), :] = total

    @pl.when(jnp.logical_not(spill))
    def _():
        def patch(k, lead_ref, rows):
            near = others(k)
            for n in range(0, 9, 2):
                p, px, py = near[n]
                cols = moved(fu_ref[p], px, py, STEP_H)
                if n < 8:
                    r, rx, ry = near[n + 1]
                    cols = jnp.where(half, cols, moved(turn_ref[r], rx, ry, STEP_H))
                else:
                    cols = jnp.where(half, cols, fj_ref[k + PX])
                pull = pair_block(lead_ref, cols, others_than(64, 64) if n == 8 else None)
                for d in range(3):
                    if n == 0:
                        sumf_ref[d, rows] = pull[d]
                    else:
                        sumf_ref[d, rows] += pull[d]
                    back = fold8(pull[d])
                    acc_ref[p, 8 * d : 8 * d + 8, :] -= back
                    if n < 8:
                        accr_ref[r, 8 * d : 8 * d + 8, :] -= back

        def finish_two(k):
            for d in range(3):
                total = jnp.sum(sumf_ref[d].T, axis=0, keepdims=True)
                own_ref[d, pl.ds(k, 1), :] = jnp.where(half[0:1], 0.0, pltpu.roll(total, 64, 1))
                own_ref[d, pl.ds(k + 1, 1), :] = jnp.where(half[0:1], 0.0, total)

        def two(t, carry):
            k = 2 * t
            spread(fj_ref[k + 1 + PX], leads[1], 64)
            finish_two((k + OWN - 2) % OWN)
            patch(k, leads[0], slice(0, 64))
            spread(fj_ref[k + 2 + PX], leads[0], 64)
            patch(k + 1, leads[1], slice(64, 128))
            return carry

        spread(fj_ref[PX], leads[0], 64)
        sumf_ref[...] = jnp.zeros(sumf_ref.shape, F32)
        lax.fori_loop(0, OWN // 2, two, 0)
        finish_two(OWN - 2)

    @pl.when(spill)
    def _():
        def one(k, carry):
            spread(fj_ref[k + PX], full_ref, 128)
            cols = jnp.where(jnp.logical_and(half, row8 == 0), -FAR, fj_ref[k + PX])
            for n, (p, px, py) in enumerate(others(k)):
                pull = pair_block(full_ref, moved(fu_ref[p], px, py, STEP_H))
                for d in range(3):
                    if n == 0:
                        sumf_ref[d] = pull[d]
                    else:
                        sumf_ref[d] += pull[d]
                    acc_ref[p, 8 * d : 8 * d + 8, :] -= fold8(pull[d])
            pull = pair_block(full_ref, cols, others_than(64, 64), slice(64, 128))
            for d in range(3):
                sumf_ref[d, 64:128] += pull[d]
            finish(k, sumf_ref, 128)
            return carry

        lax.fori_loop(0, OWN, one, 0)

    @pl.when(jnp.logical_not(spill))
    def _():
        def one(p, carry):
            for d in range(3):
                rows = slice(8 * d, 8 * d + 8)
                total = acc_ref[p, rows, :] + pltpu.roll(accr_ref[p, rows, :], 64, 1)
                total = jnp.sum(jnp.where(half, total, 0.0), axis=0, keepdims=True)
                up_ref[d, pl.ds(p, 1), :] = total
            return carry

        lax.fori_loop(0, EXT, one, 0, unroll=16)

    @pl.when(spill)
    def _():
        def one(p, carry):
            for d in range(3):
                up_ref[d, pl.ds(p, 1), :] = fold(acc_ref, p, d)
            return carry

        lax.fori_loop(0, EXT, one, 0)


def last_kernel(
    fj_ref,
    first_ref,
    rise_ref,
    up_ref,
    rank_ref,
    force_ref,
    own_ref,
    lead0_ref,
    lead1_ref,
    sum0_ref,
    sum1_ref,
    acc_ref,
    came_ref,
    parts_ref,
    up_send,
    up_recv,
    part_send,
    part_recv,
):
    group = lax.axis_index("patch")
    groups = lax.axis_size("patch")
    below = lax.rem(group + groups - 1, groups)
    above = lax.rem(group + 1, groups)
    me = lax.axis_index("sub")
    barrier = pltpu.get_barrier_semaphore()
    pl.semaphore_signal(barrier, inc=1, device_id={"patch": below}, device_id_type=MESH)
    for step in range(1, SUBS):
        peer = lax.rem(me + step, SUBS)
        pl.semaphore_signal(barrier, inc=1, device_id={"sub": peer}, device_id_type=MESH)
    clear(acc_ref, own_ref)
    work = (fj_ref, (lead0_ref, lead1_ref), (sum0_ref, sum1_ref), acc_ref, own_ref)
    plane_patches(SECOND, THIRD, *work)
    pl.semaphore_wait(barrier, SUBS)
    raised = pltpu.make_async_remote_copy(
        src_ref=up_ref,
        dst_ref=came_ref,
        send_sem=up_send,
        recv_sem=up_recv,
        device_id={"patch": above},
        device_id_type=MESH,
    )
    raised.start()
    plane_patches(THIRD, OWN, *work)
    add_folded(acc_ref, own_ref)
    for d in range(3):
        own_ref[d] += first_ref[d]
        own_ref[d, PX : PX + OWN, :] += rise_ref[d]
    slot = lax.broadcasted_iota(jnp.int32, (128, 128), 0).astype(F32)
    row8 = lax.broadcasted_iota(jnp.int32, (8, 128), 0)
    raised.wait()

    def unsort(k, carry):
        hit = (rank_ref[pl.ds(k, 1), :] == slot).astype(F32).astype(BF16)
        tile = [own_ref[d, pl.ds(k, 1), :] + came_ref[d, pl.ds(k, 1), :] for d in range(3)]
        tile = jnp.where(row8 == 0, tile[0], jnp.where(row8 == 1, tile[1], tile[2]))
        total = jnp.dot(stacked(tile), hit, preferred_element_type=F32)
        total = total[0:8] + total[8:16] + total[16:24]
        for d in range(3):
            parts_ref[me, d, pl.ds(k, 1), :] = total[d : d + 1, :]
        return carry

    copies = []
    for piece in range(PIECES):
        rows = pl.ds(piece * (EXT // PIECES), EXT // PIECES)
        lax.fori_loop(piece * (EXT // PIECES), (piece + 1) * (EXT // PIECES), unsort, 0, unroll=16)
        for step in range(1, SUBS):
            copy = pltpu.make_async_remote_copy(
                src_ref=parts_ref.at[me, :, rows],
                dst_ref=parts_ref.at[me, :, rows],
                send_sem=part_send.at[piece, step - 1],
                recv_sem=part_recv.at[piece, step - 1],
                device_id={"sub": lax.rem(me + step, SUBS)},
                device_id_type=MESH,
            )
            copy.start()
            copies.append(copy)
    for copy in copies:
        copy.wait()
    for s in range(SUBS):
        for d in range(3):
            force = parts_ref[s, d, PX : PX + OWN, :]
            head = parts_ref[(s + SUBS - 1) % SUBS, d, PX + OWN : EXT, :]
            tail = parts_ref[(s + 1) % SUBS, d, 0:PX, :]
            force = jnp.concatenate([force[0:8] + head, force[8:24], force[24:32] + tail], axis=0)
            force_ref[d, s * OWN : (s + 1) * OWN, :] = force


VM = pl.BlockSpec(memory_space=pltpu.VMEM)


def shape(*dims, dtype=F32):
    return jax.ShapeDtypeStruct(dims, dtype)


def work_shapes(rows):
    lead = pltpu.VMEM((6, rows, 128), F32)
    total = pltpu.VMEM((3, rows, 128), F32)
    return [lead, lead, total, total, pltpu.VMEM((EXT, 24, 128), F32)]


def first_call(atoms, patch_fill, *tables):
    return pl.pallas_call(
        first_kernel,
        out_shape=(
            shape(EXT, 8, 128),
            shape(EXT, 8, 128),
            shape(EXT, 128),
            shape(3, EXT, 128),
            shape(128, 128),
        ),
        in_specs=[pl.BlockSpec(memory_space=pltpu.HBM)] * 5,
        out_specs=(VM,) * 5,
        scratch_shapes=[pltpu.VMEM((1024, 128), F32), pltpu.VMEM((128, 128), F32)]
        + work_shapes(128)
        + [
            pltpu.VMEM((5, 128, 128), F32),
            pltpu.VMEM((1, 128), jnp.int32),
            pltpu.VMEM((1, 8), F32),
            pltpu.VMEM((1, 8), F32),
            pltpu.VMEM((1, 8), F32),
            pltpu.SemaphoreType.DMA((5,)),
            pltpu.SemaphoreType.DMA,
            pltpu.SemaphoreType.DMA,
        ],
        compiler_params=pltpu.CompilerParams(
            vmem_limit_bytes=VMEM_BYTES, collective_id=0, has_side_effects=True
        ),
    )(atoms, patch_fill[None], *(table[None] for table in tables))


def up_call(features, above):
    return pl.pallas_call(
        up_kernel,
        out_shape=(shape(3, EXT, 128), shape(3, OWN, 128)),
        in_specs=[VM] * 2,
        out_specs=(VM, VM),
        scratch_shapes=[pltpu.VMEM((EXT, 8, 128), F32)]
        + work_shapes(64)
        + [pltpu.VMEM((EXT, 24, 128), F32), pltpu.VMEM((6, 128, 128), F32), pltpu.VMEM((3, 128, 128), F32)],
        compiler_params=pltpu.CompilerParams(vmem_limit_bytes=VMEM_BYTES),
    )(features, above)


def last_call(features, first, rise, up, rank):
    return pl.pallas_call(
        last_kernel,
        out_shape=shape(3, 128, 128),
        in_specs=[VM] * 5,
        out_specs=VM,
        scratch_shapes=[pltpu.VMEM((3, EXT, 128), F32)]
        + work_shapes(128)
        + [
            pltpu.VMEM((3, EXT, 128), F32),
            pltpu.VMEM((SUBS, 3, EXT, 128), F32),
            pltpu.SemaphoreType.DMA,
            pltpu.SemaphoreType.DMA,
            pltpu.SemaphoreType.DMA((PIECES, SUBS - 1)),
            pltpu.SemaphoreType.DMA((PIECES, SUBS - 1)),
        ],
        compiler_params=pltpu.CompilerParams(
            vmem_limit_bytes=VMEM_BYTES, collective_id=1, has_side_effects=True
        ),
    )(features, first, rise, up, rank)


def local(
    positions,
    velocities,
    charges,
    atom_type,
    patch_fill,
    sigma_table,
    eps_table,
    inv_mass_table,
    pair_first,
    pair_second,
):
    plane = lax.broadcasted_iota(jnp.int32, (5, 128, 128), 0)
    atoms = jnp.where(plane == 3, charges[None], atom_type.astype(F32)[None])
    atoms = jnp.where(plane < 3, jnp.pad(positions, ((0, 2), (0, 0), (0, 0))), atoms)
    features, above, rank, first, kick = first_call(
        atoms, patch_fill, sigma_table, eps_table, inv_mass_table
    )
    up, rise = up_call(features, above)
    forces = last_call(features, first, rise, up, rank)
    new_velocities = velocities + kick[None] * forces
    new_positions = positions + new_velocities
    return (new_velocities, new_positions)


def solution(mesh):
    return jax.shard_map(
        local,
        mesh=mesh,
        in_specs=(
            P(None, "patch", None),
            P(None, "patch", None),
            P("patch", None),
            P("patch", None),
            P("patch"),
            P(),
            P(),
            P(),
            P("patch", "sub", None),
            P("patch", "sub", None),
        ),
        out_specs=(P(None, "patch", None), P(None, "patch", None)),
        check_vma=False,
    )
```
